256 devices in a mesh: dom: 2 (over core), gx: 16 (over x, y), gy: 8 (over z).
Axes of the slice: x: 4, y: 4, z: 8, core: 2. Of those that a mesh axis runs over, the one named last changes fastest.
Arguments:
- fields: float32 [2, 4, 8, 2048, 1024], P('dom', None, None, 'gx', 'gy'), may hold values from -6 to 6
- turbine_mask: int32 [8, 2048, 1024], P(None, 'gx', 'gy'), may hold values 0 or 1
- inflow_source: int32 [1024], P('gy'), may hold values from 0 to 1023
- inflow_weight: int32 [1024], P('gy'), may hold values from 0 to 16
Outputs:
- fields_next: float32 [2, 4, 8, 2048, 1024], P('dom', None, None, 'gx', 'gy')
- inflow: float32 [32, 1024], P(('dom', 'gx'), 'gy')
The draws below stay inside these ranges and needn't reach their ends.
All inputs are finite; a program needn't handle non-finite values. No bound on the sum of `turbine_mask` on one device may be relied on, other than what follows from the above.
Results may differ from the reference program's by a relative error of at most 0.00016.
Values sent between devices are 32-bit elements; how exact they have to be, the bound alone decides.
No kernel may reach another device: no remote copies, remote signals or barrier semaphores. Data moves between devices by JAX's collectives and lax.ppermute only.
A program may use at most 192 MiB of HBM per device.

```python
import math
import jax
import jax.numpy as jnp
from jax import lax

NX = 2048
NY = 1024
NZ = 8
LEVELS = 4
CYCLES = 2
COARSE = 2


def smooth_field(key):
    smooth_sum = jnp.zeros((4, NX, NY), jnp.float32)
    cells_x = jnp.arange(NX, dtype=jnp.int32)
    cells_y = jnp.arange(NY, dtype=jnp.int32)
    for mode_index in range(3):
        mode_key = jax.random.fold_in(key, mode_index)
        count_x = jax.random.randint(jax.random.fold_in(mode_key, 1), (4,), NX // 64, NX // 16 + 1)
        count_y = jax.random.randint(jax.random.fold_in(mode_key, 2), (4,), NY // 64, NY // 16 + 1)
        sign_flip = 2 * jax.random.randint(jax.random.fold_in(mode_key, 3), (4,), 0, 2) - 1
        phases = jax.random.uniform(jax.random.fold_in(mode_key, 4), (4,), jnp.float32, 0.0, 2.0 * math.pi)
        turns_x = count_x[:, None] * cells_x[None, :] % NX
        turns_y = sign_flip[:, None] * count_y[:, None] * cells_y[None, :] % NY
        turn_angle = 2.0 * math.pi * (turns_x.astype(jnp.float32)[:, :, None] / NX + turns_y.astype(jnp.float32)[:, None, :] / NY) + phases[:, None, None]
        smooth_sum = smooth_sum + 1.2 * jnp.cos(turn_angle)
    return smooth_sum


def draw_fields(key, part):
    noise_key = jax.random.fold_in(key, 11)
    smooth_key = jax.random.fold_in(key, 12)
    shape = (2, 4, NZ, NX, NY)
    smooth = smooth_field(smooth_key)[:, None, :, :]
    noise = jax.random.normal(noise_key, shape, jnp.float32)
    precursor = noise[0]
    farm = 0.7 * noise[1] + smooth
    return jnp.clip(jnp.stack([precursor, farm]), -6.0, 6.0)


def plant(values, key, least, top_value):
    longest = values.shape.index(max(values.shape))
    spots = []
    for shift in (0, 1):
        where = [jax.random.randint(jax.random.fold_in(key, axis), (), 0, length) for axis, length in enumerate(values.shape)]
        where[longest] = (where[longest] + shift) % values.shape[longest]
        spots.append(tuple(where))
    return values.at[spots[0]].set(least).at[spots[1]].set(top_value)


def setup_inputs(seed: int = 0) -> dict:
    keys = jax.random.split(jax.random.key(seed), 5)
    return {
        "fields": draw_fields(jax.random.fold_in(keys[4], 71), 0),
        "turbine_mask": plant((jax.random.randint(keys[1], (NZ, NX, NY), 0, 8) < 1).astype(jnp.int32), jax.random.fold_in(keys[1], 1), 0, 1),
        "inflow_source": plant(jax.random.randint(keys[2], (NY,), 0, NY), jax.random.fold_in(keys[2], 1), 0, NY - 1).astype(jnp.int32),
        "inflow_weight": plant(jax.random.randint(keys[3], (NY,), 0, 17), jax.random.fold_in(keys[3], 1), 0, 16).astype(jnp.int32),
    }


time_step = 0.2
mean_wind = 1.0
viscosity = 0.05
vertical_mix = 0.1
thrust = 1.0
damping = 0.8


def spectral(values, axis_index):
    length = values.shape[axis_index]
    wavenumber = jnp.fft.fftfreq(length) * length
    spacing = 2.0 * jnp.pi / length
    first_factor = jnp.where(jnp.abs(wavenumber) * 2 == length, 0.0, wavenumber) * spacing
    second_factor = -(wavenumber * spacing) ** 2
    shaped = [1] * values.ndim
    shaped[axis_index] = length
    spectrum = jnp.fft.fft(values, axis=axis_index)
    slope_part = jnp.real(jnp.fft.ifft(spectrum * (1j * first_factor).reshape(shaped), axis=axis_index))
    bend_part = jnp.real(jnp.fft.ifft(spectrum * second_factor.reshape(shaped), axis=axis_index))
    return slope_part.astype(values.dtype), bend_part.astype(values.dtype)


def vertical(values):
    upper_cells = jnp.concatenate([values[..., 1:, :, :], values[..., -1:, :, :]], axis=-3)
    lower_cells = jnp.concatenate([values[..., :1, :, :], values[..., :-1, :, :]], axis=-3)
    return upper_cells, lower_cells


def precursor_step(current):
    def derive(component):
        slope_x, bend_x = spectral(component, 1)
        slope_y, bend_y = spectral(component, 2)
        return slope_x, bend_x, slope_y, bend_y

    slope_x, bend_x, slope_y, bend_y = lax.map(derive, current)
    upper_cells, lower_cells = vertical(current)
    part_x = -(mean_wind + current[0]) * slope_x + viscosity * bend_x
    part_y = -current[1] * slope_y + viscosity * bend_y
    part_z = -current[2] * (upper_cells - lower_cells) * 0.5 + vertical_mix * (upper_cells + lower_cells - 2.0 * current)
    return current + time_step * (part_x + part_y + part_z)


def neighbours(values, west_edge, east_edge):
    east_cells = jnp.concatenate([values[..., 1:, :], east_edge[..., None, :]], axis=-2)
    west_cells = jnp.concatenate([west_edge[..., None, :], values[..., :-1, :]], axis=-2)
    north_cells = jnp.roll(values, -1, axis=-1)
    south_cells = jnp.roll(values, 1, axis=-1)
    return east_cells, west_cells, north_cells, south_cells


def pressure_cells(pressure):
    return neighbours(pressure, pressure[..., 0, :], jnp.zeros_like(pressure[..., 0, :]))


def operate(pressure, grid_level, cells):
    east_cells, west_cells, north_cells, south_cells = cells
    upper_cells, lower_cells = vertical(pressure)
    factor = 0.25 ** grid_level
    return factor * (2.0 * pressure - east_cells - west_cells) + factor * (2.0 * pressure - north_cells - south_cells) + (2.0 * pressure - upper_cells - lower_cells)


def jacobi_sweep(pressure, target, grid_level, from_zero):
    diagonal = 4.0 * 0.25 ** grid_level + 2.0
    if from_zero:
        return damping * target / diagonal
    return pressure + damping * (target - operate(pressure, grid_level, pressure_cells(pressure))) / diagonal


def restrict(residual):
    depth, rows_count, cols_count = residual.shape
    return residual.reshape(depth, rows_count // 2, 2, cols_count // 2, 2).mean(axis=(2, 4))


def prolong(correction):
    return jnp.repeat(jnp.repeat(correction, 2, axis=1), 2, axis=2)


def vcycle(grid_level, pressure, target, from_zero):
    if grid_level == LEVELS - 1:
        for sweep_index in range(COARSE):
            pressure = jacobi_sweep(pressure, target, grid_level, from_zero and sweep_index == 0)
        return pressure
    pressure = jacobi_sweep(pressure, target, grid_level, from_zero)
    residual = target - operate(pressure, grid_level, pressure_cells(pressure))
    coarse_target = restrict(residual)
    correction = vcycle(grid_level + 1, jnp.zeros_like(coarse_target), coarse_target, True)
    pressure = pressure + prolong(correction)
    return jacobi_sweep(pressure, target, grid_level, False)


def farm_step(current, inflow, turbine_mask):
    east_cells, west_cells, north_cells, south_cells = neighbours(current, inflow, current[..., -1, :])
    upper_cells, lower_cells = vertical(current)
    moving = -(mean_wind + current[0]) * (east_cells - west_cells) * 0.5 - current[1] * (north_cells - south_cells) * 0.5 - current[2] * (upper_cells - lower_cells) * 0.5
    mixing = viscosity * (east_cells + west_cells + north_cells + south_cells - 4.0 * current) + vertical_mix * (upper_cells + lower_cells - 2.0 * current)
    flags = jnp.array([1.0, 1.0, 1.0, 0.0], current.dtype).reshape(4, 1, 1, 1)
    drag = thrust * turbine_mask.astype(current.dtype) * jnp.abs(current[0])
    star = current + time_step * (moving + mixing - drag * current * flags)
    star_east, star_west, star_north, star_south = neighbours(star[:2], inflow[:2], star[:2, ..., -1, :])
    upward = star[2]
    zero_level = jnp.zeros_like(upward[:1])
    upward_above = jnp.concatenate([upward[1:], zero_level], axis=0)
    upward_below = jnp.concatenate([zero_level, upward[:-1]], axis=0)
    source = -((star_east[0] - star_west[0]) * 0.5 + (star_north[1] - star_south[1]) * 0.5 + (upward_above - upward_below) * 0.5)
    pressure = jnp.zeros_like(source)
    for cycle_index in range(CYCLES):
        pressure = vcycle(0, pressure, source, cycle_index == 0)
    east_pressure, west_pressure, north_pressure, south_pressure = pressure_cells(pressure)
    upper_pressure, lower_pressure = vertical(pressure)
    gradient = jnp.stack([(east_pressure - west_pressure) * 0.5, (north_pressure - south_pressure) * 0.5, (upper_pressure - lower_pressure) * 0.5, jnp.zeros_like(pressure)])
    return star - gradient


def reference(fields, turbine_mask, inflow_source, inflow_weight):
    precursor = fields[0]
    inlet_plane = precursor[:, :, NX // 2, :]
    share_first = inflow_weight.astype(fields.dtype) / 16.0
    follow = ((inflow_source + 1) % NY).astype(jnp.int32)
    inflow = inlet_plane[:, :, inflow_source] * share_first + inlet_plane[:, :, follow] * (1.0 - share_first)
    precursor_next = precursor_step(precursor)
    farm_next = farm_step(fields[1], inflow, turbine_mask)
    return jnp.stack([precursor_next, farm_next]), inflow.reshape(4 * NZ, NY)
```

```python
import functools

import jax
import jax.numpy as jnp
import ml_dtypes
import numpy as np
from jax import lax
from jax.experimental import pallas as pl
from jax.experimental.pallas import tpu as pltpu
from jax.sharding import PartitionSpec as P

NX = 2048
NY = 1024
NZ = 8
BX = 128
BY = 128
HALF = 64
GX = 16
GY = 8
HALO = 48
EXT = BX + 2 * HALO
F32 = jnp.float32
BF16 = jnp.bfloat16
VMEM_BYTES = 48 * 1024 * 1024


def table_entries(length):
    offset = np.arange(length, dtype=np.float64)
    spacing = 2.0 * np.pi / length
    sign = np.where(offset % 2 == 0, 1.0, -1.0)
    angle = np.pi * offset / length
    angle[0] = 1.0
    slope = 0.5 * spacing * sign * np.cos(angle) / np.sin(angle)
    bend = -0.5 * spacing * spacing * sign / np.sin(angle) ** 2
    slope[0] = 0.0
    bend[0] = -np.pi**2 / 3.0 - spacing * spacing / 6.0
    return -0.2 * slope, 0.2 * 0.05 * bend


def split_bf16(table):
    high = table.astype(np.float32).astype(ml_dtypes.bfloat16)
    low = (table - high.astype(np.float64)).astype(np.float32).astype(ml_dtypes.bfloat16)
    return high, low


def span_tables():
    tiles = []
    i = np.arange(256)
    for d in (3, 2, 1, 0, 3, 2, 1):
        index = (256 * d + i[None, :] - i[:, None]) % NY
        tiles.append(np.concatenate([entry[index] for entry in table_entries(NY)], axis=1))
    return split_bf16(np.concatenate(tiles, axis=0))


def line_tables():
    i = np.arange(256)
    both = []
    for sign in (1.0, -1.0):
        tiles = []
        for place, d in enumerate((3, 2, 1, 0, 3, 2, 1)):
            index = 256 * d + i[:, None] - i[None, :]
            flip = 1.0 if place < 4 else sign
            tiles.append(
                np.concatenate(
                    [
                        0.5 * flip * (entry[index % NX] + sign * entry[(index + NX // 2) % NX])
                        for entry in table_entries(NX)
                    ],
                    axis=0,
                )
            )
        both.append(split_bf16(np.concatenate(tiles, axis=1)))
    return both


def kernel_call(body, outs, scratch=(), scalars=1, count=0):
    specs = [pl.BlockSpec(memory_space=pltpu.SMEM)] * scalars
    specs += [pl.BlockSpec(memory_space=pltpu.VMEM)] * count
    shapes = [jax.ShapeDtypeStruct(s, F32) for s in outs]
    return pl.pallas_call(
        body,
        out_shape=shapes,
        in_specs=specs,
        out_specs=[pl.BlockSpec(memory_space=pltpu.VMEM)] * len(outs),
        scratch_shapes=list(scratch),
        compiler_params=pltpu.CompilerParams(vmem_limit_bytes=VMEM_BYTES),
    )


def lane_index(shape):
    return lax.broadcasted_iota(jnp.int32, shape, len(shape) - 1)


def halves(values):
    high = values.astype(BF16)
    return high, (values - high.astype(F32)).astype(BF16)


def send_kernel(place, own, got, ybuf, half):
    def fill(source):
        for z in range(NZ):
            for c in range(4):
                block = source(c, z)
                ybuf[z, c * HALF : (c + 1) * HALF] = block
                half[c, z] = block

    @pl.when(place[0] == 0)
    def _():
        fill(lambda c, z: own[c, z, :HALF])

    @pl.when(place[0] == 1)
    def _():
        fill(lambda c, z: got[c, z])

    plane = jnp.concatenate([own[c, :, 0, :] for c in range(4)], axis=0)
    for g in range(GY):
        ybuf[g, 4 * HALF :] = plane


def blend_kernel(half, yin, source, weight, xbuf, inflow):
    plane = jnp.concatenate([yin[g, 4 * HALF :] for g in range(GY)], axis=1)
    rows = lax.broadcasted_iota(jnp.int32, (NY, BY), 0)
    share = weight[...].astype(F32) / 16.0
    first = source[...]
    follow = jnp.where(first == NY - 1, 0, first + 1)
    table = jnp.where(rows == first, share, 0.0) + jnp.where(rows == follow, 1.0 - share, 0.0)
    blended = jnp.dot(plane, table, precision=lax.Precision.HIGHEST, preferred_element_type=F32)
    inflow[...] = blended
    lane = lane_index((HALF, BY))
    for z in range(NZ):
        for part in range(4):
            total = None
            for c in range(4):
                shift = 32 * ((c - part) % 4)
                moved = half[c, z] if shift == 0 else pltpu.roll(half[c, z], shift, 1)
                total = moved if total is None else jnp.where(lane >= 32 * c, moved, total)
            xbuf[4 * z + part, :HALF] = total
    for r in range(4 * NZ):
        xbuf[r, HALF:] = jnp.broadcast_to(blended[r : r + 1], (8, BY))


def span_kernel(yin, table_high, table_low, yout, high, low):
    for g in range(GY):
        h, l = halves(yin[g, : 4 * HALF])
        high[:, g * BY : (g + 1) * BY] = h
        low[:, g * BY : (g + 1) * BY] = l
    for i in range(4):
        at = pl.ds((3 - i) * 256, 4 * 256)
        th = table_high[at, :]
        value = jnp.dot(high[...], th, preferred_element_type=F32)
        value += jnp.dot(low[...], th, preferred_element_type=F32)
        value += jnp.dot(high[...], table_low[at, :], preferred_element_type=F32)
        for k in range(2):
            g = 2 * i + k
            v = yin[g, HALF : 2 * HALF]
            for c in range(4):
                rows = slice(c * HALF, (c + 1) * HALF)
                yout[g, rows] = (
                    v * value[rows, k * BY : (k + 1) * BY]
                    + value[rows, 256 + k * BY : 256 + (k + 1) * BY]
                )


def chunk_place(m):
    return (m % 2) * GX + m // 2


def line_kernel(xin, sh, sl, ah, al, xout, plus_h, plus_l, minus_h, minus_l):
    for m in range(16):
        a = xin[chunk_place(m), :HALF]
        b = xin[chunk_place(m + 16), :HALF]
        rows = slice(m * HALF, (m + 1) * HALF)
        plus_h[rows], plus_l[rows] = halves(a + b)
        minus_h[rows], minus_l[rows] = halves(a - b)
    lane = lane_index((HALF, BY))
    for i in range(4):
        at = pl.ds((3 - i) * 256, 4 * 256)

        def product(table_high, table_low, high, low):
            th = table_high[:, at]
            value = jnp.dot(th, high[...], preferred_element_type=F32)
            value += jnp.dot(th, low[...], preferred_element_type=F32)
            return value + jnp.dot(table_low[:, at], high[...], preferred_element_type=F32)

        even = product(sh, sl, plus_h, plus_l)
        odd = product(ah, al, minus_h, minus_l)
        for k in range(4):
            for side, value in ((0, even + odd), (1, even - odd)):
                place = chunk_place(4 * i + k + 16 * side)
                u = jnp.where(lane < 32, xin[place, :HALF], 0.0)
                u = u + pltpu.roll(u, 32, 1)
                u = u + pltpu.roll(u, 64, 1)
                rows = slice(k * HALF, (k + 1) * HALF)
                late = slice(256 + k * HALF, 256 + (k + 1) * HALF)
                xout[place] = (1.0 + u) * value[rows] + value[late]


def finish_kernel(half, yback, xback, out):
    lane = lane_index((HALF, BY))
    for z in range(NZ):
        for c in range(4):
            total = None
            for part in range(4):
                shift = 32 * ((part - c) % 4)
                tile = xback[4 * z + part]
                moved = tile if shift == 0 else pltpu.roll(tile, shift, 1)
                total = moved if total is None else jnp.where(lane >= 32 * part, moved, total)
            q = half[c, z]
            upper = half[c, min(z + 1, NZ - 1)]
            lower = half[c, max(z - 1, 0)]
            mixed = 0.02 * (upper + lower - 2.0 * q) - 0.1 * half[2, z] * (upper - lower)
            out[c, z] = q + total + yback[z, c * HALF : (c + 1) * HALF] + mixed


def turn_kernel(place, own, mask, cells, drag, row_low, row_high, col_low, col_high):
    @pl.when(place[0] == 1)
    def _():
        for z in range(NZ):
            for c in range(4):
                cells[c, pl.ds(z, BX, stride=NZ), :] = own[c, z]
            drag[pl.ds(z, BX, stride=NZ), :] = mask[z].astype(F32)
        for c in range(4):
            row_low[c] = cells[c, :NZ]
            row_high[c] = cells[c, (BX - 1) * NZ :]
        lane = lane_index((NZ, BY))

        def step(x, carry):
            low, high = carry
            hit = lane == x
            at = pl.ds(pl.multiple_of(x * NZ, NZ), NZ)
            low = tuple(jnp.where(hit, cells[c, at, 0:1], low[c]) for c in range(4))
            high = tuple(jnp.where(hit, cells[c, at, BY - 1 :], high[c]) for c in range(4))
            return low, high

        zero = tuple(jnp.zeros((NZ, BY), F32) for _ in range(4))
        low, high = lax.fori_loop(0, BX, step, (zero, zero), unroll=4)
        for c in range(4):
            col_low[c] = low[c]
            col_high[c] = high[c]


def above_below(p):
    z = lax.broadcasted_iota(jnp.int32, p.shape, p.ndim - 2)
    above = jnp.where(z == NZ - 1, p, pltpu.roll(p, NZ - 1, p.ndim - 2))
    below = jnp.where(z == 0, p, pltpu.roll(p, 1, p.ndim - 2))
    return above, below


def star_kernel(place, cells, drag, ghost_w, ghost_e, ghost_s, ghost_n, inflow,
                star, partial, strip_s, strip_n, wide):
    @pl.when(place[0] == 1)
    def _():
        first = place[1] == 0
        last = place[1] == GX - 1
        lane = lane_index((NZ, BY))
        level = lax.broadcasted_iota(jnp.int32, (NZ, BY), 0)

        def star_row(x, west_of, east_of):
            u = cells[0, x]
            v = 0.5 * cells[1, x]
            w = 0.5 * cells[2, x]
            fast = 0.5 * (1.0 + u)
            push = drag[x] * jnp.abs(u)
            for c in range(4):
                f = cells[c, x]
                west = west_of(c)
                east = east_of(c)
                north = jnp.where(
                    lane == BY - 1,
                    pltpu.roll(ghost_n[c], BY - 1 - x, 1),
                    pltpu.roll(f, BY - 1, 1),
                )
                south = jnp.where(
                    lane == 0, pltpu.roll(ghost_s[c], (BY - x) % BY, 1), pltpu.roll(f, 1, 1)
                )
                above, below = above_below(f)
                moving = -fast * (east - west) - v * (north - south) - w * (above - below)
                mixing = 0.05 * (east + west + north + south - 4.0 * f) + 0.1 * (
                    above + below - 2.0 * f
                )
                total = moving + mixing
                if c < 3:
                    total = total - push * f
                star[c, x] = f + 0.2 * total

        star_row(
            0, lambda c: jnp.where(first, inflow[c], ghost_w[c]), lambda c: cells[c, 1]
        )

        def star_rows(x, carry):
            star_row(x, lambda c: cells[c, x - 1], lambda c: cells[c, x + 1])
            return carry

        lax.fori_loop(1, BX - 1, star_rows, 0, unroll=6)
        star_row(
            BX - 1,
            lambda c: cells[c, BX - 2],
            lambda c: jnp.where(last, cells[c, BX - 1], ghost_e[c]),
        )

        def source_row(x, west, east):
            v = star[1, x]
            north = jnp.where(lane == BY - 1, 0.0, pltpu.roll(v, BY - 1, 1))
            south = jnp.where(lane == 0, 0.0, pltpu.roll(v, 1, 1))
            w = star[2, x]
            above = jnp.where(level == NZ - 1, 0.0, pltpu.roll(w, NZ - 1, 0))
            below = jnp.where(level == 0, 0.0, pltpu.roll(w, 1, 0))
            total = -0.5 * ((east - west) + (north - south) + (above - below))
            partial[x] = total
            wide[0, x] = jnp.where(lane == HALF - 1, v[:, 0:1], total)
            wide[1, x] = jnp.where(lane == HALF, v[:, BY - 1 :], total)

        source_row(0, jnp.where(first, inflow[0], 0.0), star[0, 1])

        def source_rows(x, carry):
            source_row(x, star[0, x - 1], star[0, x + 1])
            return carry

        lax.fori_loop(1, BX - 1, source_rows, 0, unroll=6)
        source_row(BX - 1, star[0, BX - 2], jnp.where(last, star[0, BX - 1], 0.0))
        for k in range(2):
            wide[k, BX] = star[0, 0]
            wide[k, BX + 1] = star[0, BX - 1]

        def fold(k, carry):
            early_s, late_s = wide[0, k], wide[0, k + 65]
            strip_s[k] = jnp.where(lane < HALF, early_s, pltpu.roll(late_s, HALF, 1))
            early_n, late_n = wide[1, k], wide[1, k + 65]
            strip_n[k] = jnp.where(lane < HALF, pltpu.roll(early_n, HALF, 1), late_n)
            return carry

        lax.fori_loop(0, 65, fold, 0, unroll=13)


def widen_kernel(place, partial, star, from_s, from_n, whole, rims, send_w, send_e):
    @pl.when(place[0] == 1)
    def _():
        lane = lane_index((NZ, BY))
        near = lane < HALF

        def pieces(k, early, own):
            s, n = from_s[k], from_n[k]
            if early:
                n = pltpu.roll(n, HALF, 1)
            else:
                s = pltpu.roll(s, HALF, 1)
            turned = pltpu.roll(own, HALF, 1)
            return jnp.where(near, s, turned), jnp.where(near, turned, n)

        def rows(offset, early):
            def step(k, carry):
                x = k + offset
                a, b = pieces(k, early, partial[x])
                v = 0.5 * star[1, x]
                a = a + jnp.where(lane == HALF, 0.5 * a[:, 0:1], 0.0)
                a = a - jnp.where(lane == HALF - 1, v[:, 0:1], 0.0)
                b = b - jnp.where(lane == HALF - 1, 0.5 * b[:, BY - 1 :], 0.0)
                b = b + jnp.where(lane == HALF, v[:, BY - 1 :], 0.0)
                whole[x, :, :BY] = a
                whole[x, :, BY:] = b
                return carry

            return step

        lax.fori_loop(0, 65, rows(0, True), 0, unroll=5)
        lax.fori_loop(0, BX - 65, rows(65, False), 0, unroll=7)
        for k, x in ((0, 0), (1, BX - 1)):
            a, b = pieces(BX + k - 65, False, star[0, x])
            rims[k, :, :BY] = a
            rims[k, :, BY:] = b
        send_w[:HALO] = whole[:HALO]
        send_w[HALO] = rims[0]
        send_e[:HALO] = whole[BX - HALO :]
        send_e[HALO] = rims[1]


def loop_rows(start, count, body):
    trips = count // 4
    unroll = trips if trips <= 13 else max(d for d in range(1, 7) if trips % d == 0)

    def step(k, carry):
        body(start + 4 * k)
        return carry

    lax.fori_loop(0, trips, step, 0, unroll=unroll)


def pressure_kernel(place, whole, star, rims, from_w, from_e, out, b0, p0, q0, b1, q1,
                    b2, q2, b3, q3, turned):
    targets = [b0, b1, b2, b3]
    results = [q0, q1, q2, q3]

    @pl.when(place[0] == 1)
    def _():
        first = place[1] == 0
        last = place[1] == GX - 1
        b0[:HALO] = from_w[:HALO]
        b0[HALO : HALO + BX] = whole[...]
        b0[HALO + BX :] = from_e[:HALO]
        b0[HALO] = b0[HALO] + 0.5 * from_w[HALO]
        b0[HALO - 1] = b0[HALO - 1] - 0.5 * rims[0]
        b0[HALO + BX - 1] = b0[HALO + BX - 1] - 0.5 * from_e[HALO]
        b0[HALO + BX] = b0[HALO + BX] + 0.5 * rims[1]

        def ghosts(p, level):
            low = HALO >> level
            high = low + (BX >> level)

            @pl.when(first)
            def _():
                p[low - 1] = p[low]

            @pl.when(last)
            def _():
                p[high] = jnp.zeros((NZ, 2 * BY), F32)

        def around(rows, level):
            mid = rows[1:5]
            gap = 1 << level
            side = rows[2:6] + rows[0:4] + pltpu.roll(mid, 2 * BY - gap, 2) + pltpu.roll(mid, gap, 2)
            above, below = above_below(mid)
            return mid, 0.25**level * side + (above + below)

        def diagonal(level):
            return 4.0 * 0.25**level + 2.0

        def each(level, halo, body):
            loop_rows((HALO >> level) - halo, (BX >> level) + 2 * halo, body)

        def scaled(b, level):
            scale = 0.8 / diagonal(level)
            return lambda r: scale * b[pl.ds(r - 1, 6)]

        def plain(p):
            return lambda r: p[pl.ds(r - 1, 6)]

        def raised(rows_of, e):
            def rows(r):
                add = e[pl.ds(r // 2 - 1, 4)]
                add = jnp.broadcast_to(add[:, None], (4, 2, NZ, 2 * BY)).reshape(8, NZ, 2 * BY)
                return rows_of(r) + add[1:7]

            return rows

        def sweep(rows_of, q, level, halo):
            b = targets[level]
            scale = 0.8 / diagonal(level)

            def rows(r):
                mid, near = around(rows_of(r), level)
                at = pl.ds(r, 4)
                q[at] = 0.2 * mid + scale * (b[at] + near)

            each(level, halo, rows)

        def descend(rows_of, level, halo):
            b = targets[level]
            coarse = targets[level + 1]
            gap = 1 << level

            def rows(r):
                mid, near = around(rows_of(r), level)
                rest = b[pl.ds(r, 4)] - diagonal(level) * mid + near
                rest = rest.reshape(2, 2, NZ, 2 * BY)
                pair = rest[:, 0] + rest[:, 1]
                lane = lane_index(pair.shape)
                other = jnp.where(
                    (lane & gap) == 0,
                    pltpu.roll(pair, 2 * BY - gap, 2),
                    pltpu.roll(pair, gap, 2),
                )
                coarse[pl.ds(r // 2, 2)] = 0.25 * (pair + other)

            each(level, halo, rows)
            ghosts(coarse, level + 1)

        def cycle(level, rows_of, down, up):
            if level == 3:
                sweep(rows_of, q3, 3, up[3])
                return
            descend(rows_of, level, down[level])
            cycle(level + 1, scaled(targets[level + 1], level + 1), down, up)
            ghosts(results[level + 1], level + 1)
            sweep(raised(rows_of, results[level + 1]), results[level], level, up[level])

        ghosts(b0, 0)
        cycle(0, scaled(b0, 0), (46, 22, 10), (24, 16, 8, 4))
        ghosts(q0, 0)
        sweep(plain(q0), p0, 0, 24)
        ghosts(p0, 0)
        cycle(0, plain(p0), (24, 10, 4), (2, 4, 2, 2))
        ghosts(q0, 0)

        def final(k, carry):
            r = HALO + 4 * k
            rows = q0[pl.ds(r - 1, 6)]
            mid = rows[1:5]

            def inner(values, shift):
                return pltpu.roll(values, shift, 2)[:, :, :BY]

            grad_x = inner(0.5 * (rows[2:6] - rows[0:4]), 2 * BY - HALF)
            grad_y = 0.5 * (inner(mid, 2 * BY - HALF - 1) - inner(mid, 2 * BY - HALF + 1))
            above, low = above_below(mid)
            grad_z = inner(0.5 * (above - low), 2 * BY - HALF)
            at = pl.ds(4 * k, 4)
            to = pl.ds(pl.multiple_of(4 * NZ * k, 4 * NZ), 4 * NZ)
            turned[0, to] = (star[0, at] - grad_x).reshape(4 * NZ, BY)
            turned[1, to] = (star[1, at] - grad_y).reshape(4 * NZ, BY)
            turned[2, to] = (star[2, at] - grad_z).reshape(4 * NZ, BY)
            turned[3, to] = star[3, at].reshape(4 * NZ, BY)
            return carry

        lax.fori_loop(0, BX // 4, final, 0, unroll=4)
        for c in range(4):
            for z in range(NZ):
                out[c, z] = turned[c, pl.ds(z, BX, stride=NZ), :]


def in_step(*arrays):
    return lax.optimization_barrier(arrays)


AXES = ("dom", "gx", "gy")


def farm_device(gx, gy):
    return (GX + gx) * GY + gy


def along_y(step):
    return [
        (farm_device(a, b), farm_device(a, (b + step) % GY)) for a in range(GX) for b in range(GY)
    ]


def along_x(step):
    return [
        (farm_device(a, b), farm_device(a + step, b))
        for a in range(GX)
        for b in range(GY)
        if 0 <= a + step < GX
    ]


def on_device(fields, turbine_mask, inflow_source, inflow_weight):
    own = fields[0]
    dom = lax.axis_index("dom")
    place = jnp.stack([dom, lax.axis_index("gx")]).astype(jnp.int32)
    span_high, span_low = [jnp.asarray(t) for t in span_tables()]
    (sh, sl), (ah, al) = line_tables()
    sh, sl, ah, al = [jnp.asarray(t) for t in (sh, sl, ah, al)]
    block = (4, BX, NZ, BY)

    got = lax.ppermute(own[:, :, HALF:], "dom", [(0, 1)])
    ybuf, half = kernel_call(
        send_kernel, [(GY, 288, BY), (4, NZ, HALF, BY)], count=2
    )(place, own, got)
    cells, drag, row_low, row_high, col_low, col_high = kernel_call(
        turn_kernel, [(4, BX * NZ, BY), (BX * NZ, BY)] + [(4, NZ, BY)] * 4, count=2
    )(place, own, turbine_mask)
    cells = cells.reshape(block)
    drag = drag.reshape(BX, NZ, BY)
    yin = lax.all_to_all(ybuf, "gy", 0, 0, tiled=True)
    ghost_e = lax.ppermute(row_low, AXES, along_x(-1))
    ghost_w = lax.ppermute(row_high, AXES, along_x(1))
    ghost_n = lax.ppermute(col_low, AXES, along_y(-1))
    ghost_s = lax.ppermute(col_high, AXES, along_y(1))

    yin, cells, drag, ghost_e, ghost_w, ghost_n, ghost_s = in_step(
        yin, cells, drag, ghost_e, ghost_w, ghost_n, ghost_s
    )
    xbuf, blended = kernel_call(
        blend_kernel, [(32, 72, BY), (32, BY)], scalars=0, count=4
    )(half, yin, inflow_source[None], inflow_weight[None])
    xin = lax.all_to_all(xbuf, ("dom", "gx"), 0, 0, tiled=True)
    inflow_row = xin[NX // 2 // BX, HALF : HALF + 1]
    inlet = lax.ppermute(blended, AXES, [(8 * GY + b, GX * GY + b) for b in range(GY)])
    (yout,) = kernel_call(
        span_kernel,
        [(GY, 4 * HALF, BY)],
        scratch=[pltpu.VMEM((4 * HALF, NY), BF16)] * 2,
        scalars=0,
        count=3,
    )(yin, span_high, span_low)
    star, partial, strip_s, strip_n = kernel_call(
        star_kernel,
        [block, (BX, NZ, BY), (65, NZ, BY), (65, NZ, BY)],
        scratch=[pltpu.VMEM((2, BX + 2, NZ, BY), F32)],
        count=7,
    )(place, cells, drag, ghost_w, ghost_e, ghost_s, ghost_n, inlet.reshape(4, NZ, BY))
    xin, yout, star, partial, strip_s, strip_n = in_step(
        xin, yout, star, partial, strip_s, strip_n
    )
    yback = lax.all_to_all(yout, "gy", 0, 0, tiled=True)

    from_n = lax.ppermute(strip_s, AXES, along_y(-1))
    from_s = lax.ppermute(strip_n, AXES, along_y(1))
    whole, rims, send_w, send_e = kernel_call(
        widen_kernel,
        [(BX, NZ, 2 * BY), (2, NZ, 2 * BY), (HALO + 1, NZ, 2 * BY), (HALO + 1, NZ, 2 * BY)],
        count=4,
    )(place, partial, star, from_s, from_n)
    from_e = lax.ppermute(send_w, AXES, along_x(-1))
    from_w = lax.ppermute(send_e, AXES, along_x(1))

    (xout,) = kernel_call(
        line_kernel,
        [(32, HALF, BY)],
        scratch=[pltpu.VMEM((NX // 2, BY), BF16)] * 4,
        scalars=0,
        count=5,
    )(xin, sh, sl, ah, al)
    yback, xout, whole, rims, from_w, from_e = in_step(yback, xout, whole, rims, from_w, from_e)
    xback = lax.all_to_all(xout, ("dom", "gx"), 0, 0, tiled=True)
    (farm_next,) = kernel_call(
        pressure_kernel,
        [(4, NZ, BX, BY)],
        scratch=[
            pltpu.VMEM((EXT >> level, NZ, 2 * BY), F32) for level in (0, 0, 0, 1, 1, 2, 2, 3, 3)
        ]
        + [pltpu.VMEM((4, BX * NZ, BY), F32)],
        count=5,
    )(place, whole, star, rims, from_w, from_e)

    xback, farm_next = in_step(xback, farm_next)
    (mine,) = kernel_call(finish_kernel, [(4, NZ, HALF, BY)], scalars=0, count=3)(
        half, yback, xback
    )
    theirs = lax.ppermute(mine, "dom", [(1, 0)])
    combined = jnp.where(dom == 0, jnp.concatenate([mine, theirs], axis=2), farm_next)
    return combined[None], inflow_row


def solution(mesh):
    placed = (P("dom", None, None, "gx", "gy"), P(None, "gx", "gy"), P("gy"), P("gy"))
    return jax.shard_map(
        on_device,
        mesh=mesh,
        in_specs=placed,
        out_specs=(P("dom", None, None, "gx", "gy"), P(("dom", "gx"), "gy")),
        check_vma=False,
    )
```

```python
import functools

import jax
import jax.numpy as jnp
import ml_dtypes
import numpy as np
from jax import lax
from jax.experimental import pallas as pl
from jax.experimental.pallas import tpu as pltpu
from jax.sharding import PartitionSpec as P

NX = 2048
NY = 1024
NZ = 8
BX = 128
BY = 128
HALF = 64
GX = 16
GY = 8
HALO = 48
FX = 64
FOLD = FX // 2 + 1
EXT = FX + 2 * HALO
F32 = jnp.float32
BF16 = jnp.bfloat16
VMEM_BYTES = 63 * 1024 * 1024


def table_entries(length):
    offset = np.arange(length, dtype=np.float64)
    spacing = 2.0 * np.pi / length
    sign = np.where(offset % 2 == 0, 1.0, -1.0)
    angle = np.pi * offset / length
    angle[0] = 1.0
    slope = 0.5 * spacing * sign * np.cos(angle) / np.sin(angle)
    bend = -0.5 * spacing * spacing * sign / np.sin(angle) ** 2
    slope[0] = 0.0
    bend[0] = -np.pi**2 / 3.0 - spacing * spacing / 6.0
    return -0.2 * slope, 0.2 * 0.05 * bend


def split_bf16(table):
    high = table.astype(np.float32).astype(ml_dtypes.bfloat16)
    low = (table - high.astype(np.float64)).astype(np.float32).astype(ml_dtypes.bfloat16)
    return high, low


def span_tables():
    tiles = []
    i = np.arange(256)
    for d in (3, 2, 1, 0):
        index = (256 * d + i[None, :] - i[:, None]) % NY
        tiles.append(np.concatenate([entry[index] for entry in table_entries(NY)], axis=1))
    return split_bf16(np.concatenate(tiles, axis=0))


def line_tables():
    i = np.arange(256)
    both = []
    for sign in (1.0, -1.0):
        tiles = []
        for d in (3, 2, 1, 0):
            index = 256 * d + i[:, None] - i[None, :]
            tiles.append(
                np.concatenate(
                    [
                        0.5 * (entry[index % NX] + sign * entry[(index + NX // 2) % NX])
                        for entry in table_entries(NX)
                    ],
                    axis=0,
                )
            )
        both.append(split_bf16(np.concatenate(tiles, axis=1)))
    return both


def staged_call(body, ins, outs, scratch=(), gate=None, late=()):
    n, m, k = len(ins), len(outs), len(scratch)

    def kernel(place, *refs):
        far_in, far_out = refs[:n], refs[n : n + m]
        near_in = refs[n + m : 2 * n + m]
        near_out = refs[2 * n + m : 2 * n + 2 * m]
        extra = refs[2 * n + 2 * m : 2 * n + 2 * m + k]
        sem_in, sem_out = refs[2 * n + 2 * m + k :]

        def run():
            loads = [
                pltpu.make_async_copy(far_in[i], near_in[i], sem_in.at[i]) for i in range(n)
            ]
            for load in loads:
                load.start()
            for i in range(n):
                if i not in late:
                    loads[i].wait()
            waits = [loads[i].wait for i in late]
            body(place, *waits, *near_in, *near_out, *extra)
            stores = [
                pltpu.make_async_copy(near_out[i], far_out[i], sem_out.at[i]) for i in range(m)
            ]
            for store in stores:
                store.start()
            for store in stores:
                store.wait()

        if gate is None:
            run()
        else:
            pl.when(place[0] == gate)(run)

    return raw_call(
        kernel,
        n,
        outs,
        [pltpu.VMEM(x.shape, x.dtype) for x in ins]
        + [pltpu.VMEM(shape, F32) for shape in outs]
        + list(scratch)
        + [pltpu.SemaphoreType.DMA((n,)), pltpu.SemaphoreType.DMA((m,))],
    )


def raw_call(kernel, count, outs, scratch, aliases=None):
    return pl.pallas_call(
        kernel,
        out_shape=[jax.ShapeDtypeStruct(shape, F32) for shape in outs],
        in_specs=[pl.BlockSpec(memory_space=pltpu.SMEM)]
        + [pl.BlockSpec(memory_space=pl.ANY)] * count,
        out_specs=[pl.BlockSpec(memory_space=pl.ANY)] * len(outs),
        scratch_shapes=list(scratch),
        input_output_aliases=aliases or {},
        compiler_params=pltpu.CompilerParams(vmem_limit_bytes=VMEM_BYTES),
    )


def near_call(body, outs, limit, scratch=()):
    def call(place, *operands):
        return pl.pallas_call(
            body,
            out_shape=[jax.ShapeDtypeStruct(shape, F32) for shape in outs],
            in_specs=[pl.BlockSpec(memory_space=pltpu.SMEM)]
            + [pl.BlockSpec(memory_space=pltpu.VMEM)] * len(operands),
            out_specs=[pl.BlockSpec(memory_space=pltpu.VMEM)] * len(outs),
            scratch_shapes=list(scratch),
            compiler_params=pltpu.CompilerParams(vmem_limit_bytes=limit * 1024 * 1024),
        )(place, *operands)

    return call


def lane_index(shape):
    return lax.broadcasted_iota(jnp.int32, shape, len(shape) - 1)


def halves(values):
    high = values.astype(BF16)
    return high, (values - high.astype(F32)).astype(BF16)


def lead_kernel(place, own, other, column):
    @pl.when(place[0] == 0)
    def _():
        other[...] = own[:, :, HALF:]

    @pl.when(place[0] == 1)
    def _():
        other[...] = own[:, :, :HALF]

    column[...] = own[:, :, 0, :]


def load_half(place, own, got, half, sem):
    @pl.when(place[0] == 0)
    def _():
        copy = pltpu.make_async_copy(own.at[:, :, pl.ds(0, HALF)], half, sem)
        copy.start()
        copy.wait()

    @pl.when(place[0] == 1)
    def _():
        copy = pltpu.make_async_copy(got, half, sem)
        copy.start()
        copy.wait()


def run_all(copies):
    for copy in copies:
        copy.start()
    return copies


def wait_all(copies):
    for copy in copies:
        copy.wait()


def send_kernel(place, own, got, column, ybuf):
    def fill(half):
        for z in range(NZ):
            for c in range(4):
                ybuf[z, c * HALF : (c + 1) * HALF] = half(c, z)

    pl.when(place[0] == 0)(lambda: fill(lambda c, z: own[c, z, :HALF]))
    pl.when(place[0] == 1)(lambda: fill(lambda c, z: got[c, z]))
    for c in range(4):
        piece = jnp.where(place[1] == 0, column[c], own[c, :, 0, :])
        for g in range(GY):
            ybuf[g, 4 * HALF + c * NZ : 4 * HALF + (c + 1) * NZ] = piece


def pack_kernel(place, own, got, xbuf_far, half, xbuf, sem):
    load_half(place, own, got, half, sem.at[8])
    lane = lane_index((HALF, BY))
    stores = []
    for z in range(NZ):
        for part in range(4):
            total = None
            for c in range(4):
                shift = 32 * ((c - part) % 4)
                moved = half[c, z] if shift == 0 else pltpu.roll(half[c, z], shift, 1)
                total = moved if total is None else jnp.where(lane >= 32 * c, moved, total)
            xbuf[4 * z + part] = total
        tiles = pl.ds(4 * z, 4)
        stores += run_all(
            [
                pltpu.make_async_copy(
                    xbuf.at[tiles], xbuf_far.at[tiles, pl.ds(0, HALF)], sem.at[z]
                )
            ]
        )
    wait_all(stores)


def blend_kernel(place, yin, source, weight, xbuf_in, xbuf_far, inflow_far,
                 planes, first_near, weight_near, rims, inflow, sem):
    loads = run_all(
        [
            pltpu.make_async_copy(source, first_near, sem.at[0]),
            pltpu.make_async_copy(weight, weight_near, sem.at[1]),
            pltpu.make_async_copy(yin.at[:, pl.ds(4 * HALF, 4 * NZ)], planes, sem.at[2]),
        ]
    )
    wait_all(loads[:2])
    rows = lax.broadcasted_iota(jnp.int32, (NY, BY), 0)
    share = weight_near[...].astype(F32) / 16.0
    first = first_near[...]
    follow = jnp.where(first == NY - 1, 0, first + 1)
    table = jnp.where(rows == first, share, 0.0) + jnp.where(rows == follow, 1.0 - share, 0.0)
    wait_all(loads[2:])
    plane = jnp.concatenate([planes[g] for g in range(GY)], axis=1)
    blended = jnp.dot(plane, table, precision=lax.Precision.HIGHEST, preferred_element_type=F32)
    inflow[...] = blended
    for r in range(4 * NZ):
        rims[r] = jnp.broadcast_to(blended[r : r + 1], (8, BY))
    wait_all(
        run_all(
            [
                pltpu.make_async_copy(rims, xbuf_far.at[:, pl.ds(HALF, 8)], sem.at[3]),
                pltpu.make_async_copy(inflow, inflow_far, sem.at[4]),
            ]
        )
    )


def span_kernel(place, yin, table_high, table_low, yout, both):
    lines = 4 * HALF
    for g in range(GY):
        at = slice(g * BY, (g + 1) * BY)
        both[:lines, at], both[lines:, at] = halves(yin[g, :lines])
    for i in range(4):
        near = (slice(0, (i + 1) * 256), slice((3 - i) * 256, 1024))
        far = (slice((i + 1) * 256, 1024), slice(0, (3 - i) * 256))
        value = None
        for cells, rows in (near, far)[: 1 if i == 3 else 2]:
            pair = jnp.dot(both[:, cells], table_high[rows], preferred_element_type=F32)
            part = pair[:lines] + pair[lines:]
            part += jnp.dot(both[:lines, cells], table_low[rows], preferred_element_type=F32)
            value = part if value is None else value + part
        for k in range(2):
            g = 2 * i + k
            v = yin[g, HALF : 2 * HALF]
            for c in range(4):
                rows = slice(c * HALF, (c + 1) * HALF)
                yout[g, rows] = (
                    v * value[rows, k * BY : (k + 1) * BY]
                    + value[rows, 256 + k * BY : 256 + (k + 1) * BY]
                )


def chunk_place(m):
    return (m % 2) * GX + m // 2


def line_kernel(place, r0, r1, r2, r3, xin, sh, sl, ah, al, xout, inflow_row, plus, minus):
    inflow_row[...] = xin[NX // 2 // BX, HALF : HALF + 1]
    for m in range(16):
        a = xin[chunk_place(m), :HALF]
        b = xin[chunk_place(m + 16), :HALF]
        rows = slice(m * HALF, (m + 1) * HALF)
        plus[rows, :BY], plus[rows, BY:] = halves(a + b)
        minus[rows, :BY], minus[rows, BY:] = halves(a - b)
    for ready in (r0, r1, r2, r3):
        ready()
    lane = lane_index((HALF, BY))
    for i in range(4):

        def product(table_high, table_low, both, cells, columns):
            pair = jnp.dot(table_high[:, columns], both[cells], preferred_element_type=F32)
            value = pair[:, :BY] + pair[:, BY:]
            return value + jnp.dot(
                table_low[:, columns], both[cells, :BY], preferred_element_type=F32
            )

        near = (slice(0, (i + 1) * 256), slice((3 - i) * 256, 1024))
        far = (slice((i + 1) * 256, 1024), slice(0, (3 - i) * 256))
        even = product(sh, sl, plus, *near)
        odd = product(ah, al, minus, *near)
        if i < 3:
            even = even + product(sh, sl, plus, *far)
            odd = odd - product(ah, al, minus, *far)
        for k in range(4):
            for side, value in ((0, even + odd), (1, even - odd)):
                place_of = chunk_place(4 * i + k + 16 * side)
                u = jnp.where(lane < 32, xin[place_of, :HALF], 0.0)
                u = u + pltpu.roll(u, 32, 1)
                u = u + pltpu.roll(u, 64, 1)
                rows = slice(k * HALF, (k + 1) * HALF)
                late = slice(256 + k * HALF, 256 + (k + 1) * HALF)
                xout[place_of] = (1.0 + u) * value[rows] + value[late]


def finish_kernel(place, own, got, yback_far, xback_far, joined_in, send_in, joined, send,
                  half, yback, xback, out, sem):
    loads = [
        run_all(
            [
                pltpu.make_async_copy(
                    yback_far.at[pl.ds(2 * k, 2)], yback.at[pl.ds(2 * k, 2)], sem.at[1 + k]
                ),
                pltpu.make_async_copy(
                    xback_far.at[pl.ds(8 * k, 8)], xback.at[pl.ds(8 * k, 8)], sem.at[5 + k]
                ),
            ]
        )
        for k in range(4)
    ]
    load_half(place, own, got, half, sem.at[0])
    lane = lane_index((HALF, BY))
    to_own, to_other = [], []
    for k in range(4):
        at = pl.ds(2 * k, 2)
        piece = out.at[:, at]
        to_own.append(
            pltpu.make_async_copy(piece, joined.at[:, at, pl.ds(0, HALF)], sem.at[9 + k])
        )
        to_other.append(pltpu.make_async_copy(piece, send.at[:, at], sem.at[9 + k]))
    for k in range(4):
        wait_all(loads[k])
        for z in (2 * k, 2 * k + 1):
            for c in range(4):
                total = None
                for part in range(4):
                    shift = 32 * ((part - c) % 4)
                    tile = xback[4 * z + part]
                    moved = tile if shift == 0 else pltpu.roll(tile, shift, 1)
                    total = moved if total is None else jnp.where(lane >= 32 * part, moved, total)
                q = half[c, z]
                upper = half[c, min(z + 1, NZ - 1)]
                lower = half[c, max(z - 1, 0)]
                mixed = 0.02 * (upper + lower - 2.0 * q) - 0.1 * half[2, z] * (upper - lower)
                out[c, z] = q + total + yback[z, c * HALF : (c + 1) * HALF] + mixed
        pl.when(place[0] == 0)(to_own[k].start)
        pl.when(place[0] == 1)(to_other[k].start)
    pl.when(place[0] == 0)(lambda: wait_all(to_own))
    pl.when(place[0] == 1)(lambda: wait_all(to_other))


def join_kernel(place, theirs, joined_in, joined, near, sem):
    def forward(start):
        pieces = [
            (
                pltpu.make_async_copy(theirs.at[c], near.at[c], sem.at[c]),
                pltpu.make_async_copy(
                    near.at[c], joined.at[c, :, pl.ds(start, HALF)], sem.at[4 + c]
                ),
            )
            for c in range(4)
        ]
        for load, _ in pieces:
            load.start()
        for load, store in pieces:
            load.wait()
            store.start()
        for _, store in pieces:
            store.wait()

    pl.when(place[0] == 0)(lambda: forward(HALF))
    pl.when(place[0] == 1)(lambda: forward(0))


def turn_kernel(place, own, got, mask_far, cells_far, drag_far, row_low_far, row_high_far,
                col_low_far, col_high_far,
                farm, mask, cells, drag, row_low, row_high, col_low, col_high, sem):
    at_x = pl.ds(pl.multiple_of(place[0] * FX, FX), FX)
    mask_load = pltpu.make_async_copy(mask_far.at[:, at_x], mask, sem.at[1])
    mask_load.start()

    @pl.when(place[0] == 0)
    def _():
        copy = pltpu.make_async_copy(got, farm, sem.at[0])
        copy.start()
        copy.wait()

    @pl.when(place[0] == 1)
    def _():
        copy = pltpu.make_async_copy(own.at[:, :, pl.ds(FX, FX)], farm, sem.at[0])
        copy.start()
        copy.wait()

    stores = []
    for c in range(4):
        for z in range(NZ):
            cells[c, pl.ds(z, FX, stride=NZ), :] = farm[c, z]
        stores += run_all([pltpu.make_async_copy(cells.at[c], cells_far.at[c], sem.at[2 + c])])
    mask_load.wait()
    for z in range(NZ):
        drag[pl.ds(z, FX, stride=NZ), :] = mask[z].astype(F32)
    stores += run_all([pltpu.make_async_copy(drag, drag_far, sem.at[6])])
    for c in range(4):
        row_low[c] = cells[c, :NZ]
        row_high[c] = cells[c, (FX - 1) * NZ :]
    lane = lane_index((NZ, BY))

    def step(x, carry):
        low, high = carry
        hit = lane == x
        at = pl.ds(pl.multiple_of(x * NZ, NZ), NZ)
        low = tuple(jnp.where(hit, cells[c, at, 0:1], low[c]) for c in range(4))
        high = tuple(jnp.where(hit, cells[c, at, BY - 1 :], high[c]) for c in range(4))
        return low, high

    zero = tuple(jnp.zeros((NZ, BY), F32) for _ in range(4))
    low, high = lax.fori_loop(0, FX, step, (zero, zero), unroll=4)
    for c in range(4):
        col_low[c] = low[c]
        col_high[c] = high[c]
    pairs = (
        (row_low, row_low_far), (row_high, row_high_far),
        (col_low, col_low_far), (col_high, col_high_far),
    )
    stores += run_all([pltpu.make_async_copy(a, b, sem.at[7 + k]) for k, (a, b) in enumerate(pairs)])
    wait_all(stores)


def above_below(p):
    z = lax.broadcasted_iota(jnp.int32, p.shape, p.ndim - 2)
    above = jnp.where(z == NZ - 1, p, pltpu.roll(p, NZ - 1, p.ndim - 2))
    below = jnp.where(z == 0, p, pltpu.roll(p, 1, p.ndim - 2))
    return above, below


def star_kernel(place, cells, drag, ghost_w, ghost_e, ghost_s, ghost_n, inflow,
                star, partial, strip_s, strip_n, wide):
    first = place[2] == 1
    last = place[3] == 1
    lane = lane_index((NZ, BY))
    level = lax.broadcasted_iota(jnp.int32, (NZ, BY), 0)

    def star_row(x, west_of, east_of):
        u = cells[0, x]
        v = 0.5 * cells[1, x]
        w = 0.5 * cells[2, x]
        fast = 0.5 * (1.0 + u)
        push = drag[x] * jnp.abs(u)
        for c in range(4):
            f = cells[c, x]
            west = west_of(c)
            east = east_of(c)
            north = jnp.where(
                lane == BY - 1,
                pltpu.roll(ghost_n[c], BY - 1 - x, 1),
                pltpu.roll(f, BY - 1, 1),
            )
            south = jnp.where(
                lane == 0, pltpu.roll(ghost_s[c], (BY - x) % BY, 1), pltpu.roll(f, 1, 1)
            )
            above, below = above_below(f)
            moving = -fast * (east - west) - v * (north - south) - w * (above - below)
            mixing = 0.05 * (east + west + north + south - 4.0 * f) + 0.1 * (
                above + below - 2.0 * f
            )
            total = moving + mixing
            if c < 3:
                total = total - push * f
            star[c, x] = f + 0.2 * total

    star_row(
        0, lambda c: jnp.where(first, inflow[c], ghost_w[c]), lambda c: cells[c, 1]
    )

    def star_rows(x, carry):
        star_row(x, lambda c: cells[c, x - 1], lambda c: cells[c, x + 1])
        return carry

    lax.fori_loop(1, FX - 1, star_rows, 0, unroll=2)
    star_row(
        FX - 1,
        lambda c: cells[c, FX - 2],
        lambda c: jnp.where(last, cells[c, FX - 1], ghost_e[c]),
    )

    def source_row(x, west, east):
        v = star[1, x]
        north = jnp.where(lane == BY - 1, 0.0, pltpu.roll(v, BY - 1, 1))
        south = jnp.where(lane == 0, 0.0, pltpu.roll(v, 1, 1))
        w = star[2, x]
        above = jnp.where(level == NZ - 1, 0.0, pltpu.roll(w, NZ - 1, 0))
        below = jnp.where(level == 0, 0.0, pltpu.roll(w, 1, 0))
        total = -0.5 * ((east - west) + (north - south) + (above - below))
        partial[x] = total
        wide[0, x] = jnp.where(lane == HALF - 1, v[:, 0:1], total)
        wide[1, x] = jnp.where(lane == HALF, v[:, BY - 1 :], total)

    source_row(0, jnp.where(first, inflow[0], 0.0), star[0, 1])

    def source_rows(x, carry):
        source_row(x, star[0, x - 1], star[0, x + 1])
        return carry

    lax.fori_loop(1, FX - 1, source_rows, 0, unroll=2)
    source_row(FX - 1, star[0, FX - 2], jnp.where(last, star[0, FX - 1], 0.0))
    for k in range(2):
        wide[k, FX] = star[0, 0]
        wide[k, FX + 1] = star[0, FX - 1]

    def fold(k, carry):
        early_s, late_s = wide[0, k], wide[0, k + FOLD]
        strip_s[k] = jnp.where(lane < HALF, early_s, pltpu.roll(late_s, HALF, 1))
        early_n, late_n = wide[1, k], wide[1, k + FOLD]
        strip_n[k] = jnp.where(lane < HALF, pltpu.roll(early_n, HALF, 1), late_n)
        return carry

    lax.fori_loop(0, FOLD, fold, 0, unroll=11)


def widen_kernel(place, partial, star, from_s, from_n, whole, rims, send_w, send_e):
    lane = lane_index((NZ, BY))
    near = lane < HALF

    def pieces(k, early, own):
        s, n = from_s[k], from_n[k]
        if early:
            n = pltpu.roll(n, HALF, 1)
        else:
            s = pltpu.roll(s, HALF, 1)
        turned = pltpu.roll(own, HALF, 1)
        return jnp.where(near, s, turned), jnp.where(near, turned, n)

    def rows(offset, early):
        def step(k, carry):
            x = k + offset
            a, b = pieces(k, early, partial[x])
            v = 0.5 * star[1, x]
            a = a + jnp.where(lane == HALF, 0.5 * a[:, 0:1], 0.0)
            a = a - jnp.where(lane == HALF - 1, v[:, 0:1], 0.0)
            b = b - jnp.where(lane == HALF - 1, 0.5 * b[:, BY - 1 :], 0.0)
            b = b + jnp.where(lane == HALF, v[:, BY - 1 :], 0.0)
            whole[x, :, :BY] = a
            whole[x, :, BY:] = b
            return carry

        return step

    for k in range(2):
        a, b = pieces(FX + k - FOLD, False, star[0, k * (FX - 1)])
        rims[k, :, :BY] = a
        rims[k, :, BY:] = b
    lax.fori_loop(0, FOLD, rows(0, True), 0, unroll=11)
    lax.fori_loop(0, FX - FOLD, rows(FOLD, False), 0, unroll=31)
    send_w[:HALO] = whole[:HALO]
    send_w[HALO] = rims[0]
    send_e[:HALO] = whole[FX - HALO :]
    send_e[HALO] = rims[1]


def loop_rows(start, count, body):
    trips = count // 4
    unroll = trips if trips <= 19 else max(d for d in range(1, 8) if trips % d == 0)

    def step(k, carry):
        body(start + 4 * k)
        return carry

    lax.fori_loop(0, trips, step, 0, unroll=unroll)


def pressure_kernel(place, whole_far, star_far, rims_far, from_w_far, from_e_far, joined, send,
                  star, rims, far_rims, out, b0, p0, q0, b1, q1, b2, q2, b3, q3, turned, sem):
    pairs = (
        (from_w_far.at[pl.ds(0, HALO)], b0.at[pl.ds(0, HALO)]),
        (whole_far, b0.at[pl.ds(HALO, FX)]),
        (from_e_far.at[pl.ds(0, HALO)], b0.at[pl.ds(HALO + FX, HALO)]),
        (rims_far, rims),
        (from_w_far.at[HALO], far_rims.at[0]),
        (from_e_far.at[HALO], far_rims.at[1]),
    )
    loads = run_all([pltpu.make_async_copy(a, b, sem.at[k]) for k, (a, b) in enumerate(pairs)])
    (star_load,) = run_all([pltpu.make_async_copy(star_far, star, sem.at[6])])
    wait_all(loads)
    targets = [b0, b1, b2, b3]
    results = [q0, q1, q2, q3]

    first = place[2] == 1
    last = place[3] == 1
    b0[HALO] = b0[HALO] + 0.5 * far_rims[0]
    b0[HALO - 1] = b0[HALO - 1] - 0.5 * rims[0]
    b0[HALO + FX - 1] = b0[HALO + FX - 1] - 0.5 * far_rims[1]
    b0[HALO + FX] = b0[HALO + FX] + 0.5 * rims[1]

    def ghosts(p, level):
        low = HALO >> level
        high = low + (FX >> level)

        @pl.when(first)
        def _():
            p[low - 1] = p[low]

        @pl.when(last)
        def _():
            p[high] = jnp.zeros((NZ, 2 * BY), F32)

    def around(rows, level):
        mid = rows[1:5]
        gap = 1 << level
        side = rows[2:6] + rows[0:4] + pltpu.roll(mid, 2 * BY - gap, 2) + pltpu.roll(mid, gap, 2)
        above, below = above_below(mid)
        return mid, 0.25**level * side + (above + below)

    def diagonal(level):
        return 4.0 * 0.25**level + 2.0

    def each(level, halo, body):
        loop_rows((HALO >> level) - halo, (FX >> level) + 2 * halo, body)

    def scaled(b, level):
        scale = 0.8 / diagonal(level)
        return lambda r: scale * b[pl.ds(r - 1, 6)]

    def plain(p):
        return lambda r: p[pl.ds(r - 1, 6)]

    def raised(rows_of, e):
        def rows(r):
            add = e[pl.ds(r // 2 - 1, 4)]
            add = jnp.broadcast_to(add[:, None], (4, 2, NZ, 2 * BY)).reshape(8, NZ, 2 * BY)
            return rows_of(r) + add[1:7]

        return rows

    def sweep(rows_of, q, level, halo):
        b = targets[level]
        scale = 0.8 / diagonal(level)

        def rows(r):
            mid, near = around(rows_of(r), level)
            at = pl.ds(r, 4)
            q[at] = 0.2 * mid + scale * (b[at] + near)

        each(level, halo, rows)

    def descend(rows_of, level, halo):
        b = targets[level]
        coarse = targets[level + 1]
        gap = 1 << level

        def rows(r):
            mid, near = around(rows_of(r), level)
            rest = b[pl.ds(r, 4)] - diagonal(level) * mid + near
            rest = rest.reshape(2, 2, NZ, 2 * BY)
            pair = rest[:, 0] + rest[:, 1]
            lane = lane_index(pair.shape)
            other = jnp.where(
                (lane & gap) == 0,
                pltpu.roll(pair, 2 * BY - gap, 2),
                pltpu.roll(pair, gap, 2),
            )
            coarse[pl.ds(r // 2, 2)] = 0.25 * (pair + other)

        each(level, halo, rows)
        ghosts(coarse, level + 1)

    def cycle(level, rows_of, down, up):
        if level == 3:
            sweep(rows_of, q3, 3, up[3])
            return
        descend(rows_of, level, down[level])
        cycle(level + 1, scaled(targets[level + 1], level + 1), down, up)
        ghosts(results[level + 1], level + 1)
        sweep(raised(rows_of, results[level + 1]), results[level], level, up[level])

    ghosts(b0, 0)
    cycle(0, scaled(b0, 0), (46, 22, 10), (24, 14, 8, 4))
    ghosts(q0, 0)
    sweep(plain(q0), p0, 0, 24)
    ghosts(p0, 0)
    cycle(0, plain(p0), (24, 10, 4), (4, 2, 2, 2))
    ghosts(q0, 0)

    def final(k, carry):
        r = HALO + 4 * k
        rows = q0[pl.ds(r - 1, 6)]
        mid = rows[1:5]

        def inner(values, shift):
            return pltpu.roll(values, shift, 2)[:, :, :BY]

        grad_x = inner(0.5 * (rows[2:6] - rows[0:4]), 2 * BY - HALF)
        grad_y = 0.5 * (inner(mid, 2 * BY - HALF - 1) - inner(mid, 2 * BY - HALF + 1))
        above, low = above_below(mid)
        grad_z = inner(0.5 * (above - low), 2 * BY - HALF)
        at = pl.ds(4 * k, 4)
        to = pl.ds(pl.multiple_of(4 * NZ * k, 4 * NZ), 4 * NZ)
        turned[0, to] = (star[0, at] - grad_x).reshape(4 * NZ, BY)
        turned[1, to] = (star[1, at] - grad_y).reshape(4 * NZ, BY)
        turned[2, to] = (star[2, at] - grad_z).reshape(4 * NZ, BY)
        turned[3, to] = star[3, at].reshape(4 * NZ, BY)
        return carry

    star_load.wait()
    lax.fori_loop(0, FX // 4, final, 0, unroll=4)
    stores = []
    for c in range(4):
        for z in range(NZ):
            out[c, z] = turned[c, pl.ds(z, FX, stride=NZ), :]
        to_own = pltpu.make_async_copy(out.at[c], joined.at[c, :, pl.ds(FX, FX)], sem.at[7 + c])
        to_other = pltpu.make_async_copy(out.at[c], send.at[c], sem.at[7 + c])
        pl.when(place[0] == 1)(to_own.start)
        pl.when(place[0] == 0)(to_other.start)
        stores.append((to_own, to_other))
    for to_own, to_other in stores:
        pl.when(place[0] == 1)(to_own.wait)
        pl.when(place[0] == 0)(to_other.wait)


def in_step(*arrays):
    return lax.optimization_barrier(arrays)


def along_y(step):
    return [(b, (b + step) % GY) for b in range(GY)]


def along_x(step):
    count = 2 * GX
    return [
        (chunk_place(m), chunk_place(m + step)) for m in range(count) if 0 <= m + step < count
    ]


def vmem(*shapes):
    return [pltpu.VMEM(shape, F32) for shape in shapes]


def on_device(fields, turbine_mask, inflow_source, inflow_weight):
    own = fields[0]
    dom, gx = lax.axis_index("dom"), lax.axis_index("gx")
    first, last = (gx == 0) & (dom == 0), (gx == GX - 1) & (dom == 1)
    place = jnp.stack([dom, gx, first, last]).astype(jnp.int32)
    span_high, span_low = [jnp.asarray(t) for t in span_tables()]
    (sh, sl), (ah, al) = line_tables()
    sh, sl, ah, al = [jnp.asarray(t) for t in (sh, sl, ah, al)]
    block = (4, FX, NZ, BY)
    half_block = (4, NZ, HALF, BY)
    rim = (4, NZ, BY)
    strip = (FOLD, NZ, BY)
    wide_row = (NZ, 2 * BY)
    dma = pltpu.SemaphoreType.DMA
    swap = [(0, 1), (1, 0)]
    x_axes = ("dom", "gx")

    other, column = near_call(lead_kernel, [half_block, rim], 2)(place, own)
    column = lax.ppermute(column, "gx", [(NX // 2 // BX, 0)])
    got = lax.ppermute(other, "dom", swap)
    (ybuf,) = near_call(send_kernel, [(GY, 288, BY)], 2)(place, own, got, column)
    yin = lax.all_to_all(ybuf, "gy", 0, 0, tiled=True)

    cells, drag, row_low, row_high, col_low, col_high = raw_call(
        turn_kernel,
        3,
        [(4, FX * NZ, BY), (FX * NZ, BY)] + [rim] * 4,
        vmem(half_block)
        + [pltpu.VMEM((NZ, FX, BY), jnp.int32)]
        + vmem((4, FX * NZ, BY), (FX * NZ, BY), rim, rim, rim, rim)
        + [dma((11,))],
    )(place, own, got, turbine_mask)
    cells = cells.reshape(block)
    drag = drag.reshape(FX, NZ, BY)
    ghost_e = lax.ppermute(row_low, x_axes, along_x(-1))
    ghost_w = lax.ppermute(row_high, x_axes, along_x(1))
    ghost_n = lax.ppermute(col_low, "gy", along_y(-1))
    ghost_s = lax.ppermute(col_high, "gy", along_y(1))
    (xbuf,) = raw_call(
        pack_kernel, 2, [(32, 72, BY)], vmem(half_block, (32, HALF, BY)) + [dma((9,))]
    )(place, own, got)

    yin, xbuf, cells, drag, ghost_e, ghost_w, ghost_n, ghost_s = in_step(
        yin, xbuf, cells, drag, ghost_e, ghost_w, ghost_n, ghost_s
    )
    xbuf, blended = raw_call(
        blend_kernel,
        4,
        [(32, 72, BY), (4 * NZ, BY)],
        vmem((GY, 4 * NZ, BY))
        + [pltpu.VMEM((1, BY), jnp.int32)] * 2
        + vmem((32, 8, BY), (4 * NZ, BY))
        + [dma((5,))],
        {4: 0},
    )(place, yin, inflow_source[None], inflow_weight[None], xbuf)
    xin = lax.all_to_all(xbuf, x_axes, 0, 0, tiled=True)

    outs = [block, (FX, NZ, BY), strip, strip]
    star, partial, strip_s, strip_n = near_call(
        star_kernel, outs, 4, vmem((2, FX + 2, NZ, BY))
    )(place, cells, drag, ghost_w, ghost_e, ghost_s, ghost_n, blended.reshape(rim))
    from_n = lax.ppermute(strip_s, "gy", along_y(-1))
    from_s = lax.ppermute(strip_n, "gy", along_y(1))
    (yout,) = near_call(
        span_kernel, [(GY, 4 * HALF, BY)], 8, [pltpu.VMEM((8 * HALF, NY), BF16)]
    )(place, yin, span_high, span_low)
    yout, from_n, from_s = in_step(yout, from_n, from_s)
    whole, rims, send_w, send_e = near_call(
        widen_kernel,
        [(FX, *wide_row), (2, *wide_row), (HALO + 1, *wide_row), (HALO + 1, *wide_row)],
        2,
    )(place, partial, star, from_s, from_n)
    xin, yout, whole, rims, send_w, send_e = in_step(xin, yout, whole, rims, send_w, send_e)
    yback = lax.all_to_all(yout, "gy", 0, 0, tiled=True)

    from_e = lax.ppermute(send_w, x_axes, along_x(-1))
    from_w = lax.ppermute(send_e, x_axes, along_x(1))
    ins = (xin, sh, sl, ah, al)
    xout, inflow_row = staged_call(
        line_kernel,
        ins,
        [(32, HALF, BY), (1, BY)],
        scratch=[pltpu.VMEM((NX // 2, 2 * BY), BF16)] * 2,
        late=(1, 2, 3, 4),
    )(place, *ins)
    yback, xout, from_w, from_e = in_step(yback, xout, from_w, from_e)
    xback = lax.all_to_all(xout, x_axes, 0, 0, tiled=True)
    joined, send = raw_call(
        pressure_kernel,
        5,
        [(4, NZ, BX, BY), half_block],
        vmem(block, (2, *wide_row), (2, *wide_row), half_block)
        + vmem(*[(EXT >> level, *wide_row) for level in (0, 0, 0, 1, 1, 2, 2, 3, 3)])
        + vmem((4, FX * NZ, BY))
        + [dma((11,))],
    )(place, whole, star, rims, from_w, from_e)

    xback, joined, send = in_step(xback, joined, send)
    joined, send = raw_call(
        finish_kernel,
        6,
        [(4, NZ, BX, BY), half_block],
        vmem(half_block, (GY, 4 * HALF, BY), (32, HALF, BY), half_block) + [dma((13,))],
        {5: 0, 6: 1},
    )(place, own, got, yback, xback, joined, send)
    theirs = lax.ppermute(send, "dom", swap)
    (joined,) = raw_call(
        join_kernel, 2, [(4, NZ, BX, BY)], vmem(half_block) + [dma((8,))], {2: 0}
    )(place, theirs, joined)
    return joined[None], inflow_row


def solution(mesh):
    placed = (P("dom", None, None, "gx", "gy"), P(None, "gx", "gy"), P("gy"), P("gy"))
    return jax.shard_map(
        on_device,
        mesh=mesh,
        in_specs=placed,
        out_specs=(P("dom", None, None, "gx", "gy"), P(("dom", "gx"), "gy")),
        check_vma=False,
    )
```

```python
import functools

import jax
import jax.numpy as jnp
import ml_dtypes
import numpy as np
from jax import lax
from jax.experimental import pallas as pl
from jax.experimental.pallas import tpu as pltpu
from jax.sharding import PartitionSpec as P

NX = 2048
NY = 1024
NZ = 8
BX = 128
BY = 128
HALF = 64
GX = 16
GY = 8
HALO = 48
FX = 64
FOLD = FX // 2 + 1
EXT = FX + 2 * HALO
F32 = jnp.float32
BF16 = jnp.bfloat16
VMEM_BYTES = 63 * 1024 * 1024


def table_entries(length):
    offset = np.arange(length, dtype=np.float64)
    spacing = 2.0 * np.pi / length
    sign = np.where(offset % 2 == 0, 1.0, -1.0)
    angle = np.pi * offset / length
    angle[0] = 1.0
    slope = 0.5 * spacing * sign * np.cos(angle) / np.sin(angle)
    bend = -0.5 * spacing * spacing * sign / np.sin(angle) ** 2
    slope[0] = 0.0
    bend[0] = -np.pi**2 / 3.0 - spacing * spacing / 6.0
    return -0.2 * slope, 0.2 * 0.05 * bend


def split_bf16(table):
    high = table.astype(np.float32).astype(ml_dtypes.bfloat16)
    low = (table - high.astype(np.float64)).astype(np.float32).astype(ml_dtypes.bfloat16)
    return high, low


def span_tables():
    tiles = []
    i = np.arange(256)
    for d in (3, 2, 1, 0):
        index = (256 * d + i[None, :] - i[:, None]) % NY
        tiles.append(np.concatenate([entry[index] for entry in table_entries(NY)], axis=1))
    return split_bf16(np.concatenate(tiles, axis=0))


def line_tables():
    i = np.arange(256)
    both = []
    for sign in (1.0, -1.0):
        tiles = []
        for d in (3, 2, 1, 0):
            index = 256 * d + i[:, None] - i[None, :]
            tiles.append(
                np.concatenate(
                    [
                        0.5 * (entry[index % NX] + sign * entry[(index + NX // 2) % NX])
                        for entry in table_entries(NX)
                    ],
                    axis=0,
                )
            )
        both.append(split_bf16(np.concatenate(tiles, axis=1)))
    return both


def staged_call(body, ins, outs, scratch=(), gate=None, late=()):
    n, m, k = len(ins), len(outs), len(scratch)

    def kernel(place, *refs):
        far_in, far_out = refs[:n], refs[n : n + m]
        near_in = refs[n + m : 2 * n + m]
        near_out = refs[2 * n + m : 2 * n + 2 * m]
        extra = refs[2 * n + 2 * m : 2 * n + 2 * m + k]
        sem_in, sem_out = refs[2 * n + 2 * m + k :]

        def run():
            loads = [
                pltpu.make_async_copy(far_in[i], near_in[i], sem_in.at[i]) for i in range(n)
            ]
            for load in loads:
                load.start()
            for i in range(n):
                if i not in late:
                    loads[i].wait()
            waits = [loads[i].wait for i in late]
            body(place, *waits, *near_in, *near_out, *extra)
            stores = [
                pltpu.make_async_copy(near_out[i], far_out[i], sem_out.at[i]) for i in range(m)
            ]
            for store in stores:
                store.start()
            for store in stores:
                store.wait()

        if gate is None:
            run()
        else:
            pl.when(place[0] == gate)(run)

    return raw_call(
        kernel,
        n,
        outs,
        [pltpu.VMEM(x.shape, x.dtype) for x in ins]
        + [pltpu.VMEM(shape, F32) for shape in outs]
        + list(scratch)
        + [pltpu.SemaphoreType.DMA((n,)), pltpu.SemaphoreType.DMA((m,))],
    )


def raw_call(kernel, count, outs, scratch, aliases=None):
    return pl.pallas_call(
        kernel,
        out_shape=[jax.ShapeDtypeStruct(shape, F32) for shape in outs],
        in_specs=[pl.BlockSpec(memory_space=pltpu.SMEM)]
        + [pl.BlockSpec(memory_space=pl.ANY)] * count,
        out_specs=[pl.BlockSpec(memory_space=pl.ANY)] * len(outs),
        scratch_shapes=list(scratch),
        input_output_aliases=aliases or {},
        compiler_params=pltpu.CompilerParams(vmem_limit_bytes=VMEM_BYTES),
    )


def near_call(body, outs, limit, scratch=()):
    def call(place, *operands):
        return pl.pallas_call(
            body,
            out_shape=[jax.ShapeDtypeStruct(shape, F32) for shape in outs],
            in_specs=[pl.BlockSpec(memory_space=pltpu.SMEM)]
            + [pl.BlockSpec(memory_space=pltpu.VMEM)] * len(operands),
            out_specs=[pl.BlockSpec(memory_space=pltpu.VMEM)] * len(outs),
            scratch_shapes=list(scratch),
            compiler_params=pltpu.CompilerParams(vmem_limit_bytes=limit * 1024 * 1024),
        )(place, *operands)

    return call


def lane_index(shape):
    return lax.broadcasted_iota(jnp.int32, shape, len(shape) - 1)


def halves(values):
    high = values.astype(BF16)
    return high, (values - high.astype(F32)).astype(BF16)


def lead_kernel(place, own, other, column):
    @pl.when(place[0] == 0)
    def _():
        other[...] = own[:, :, HALF:]

    @pl.when(place[0] == 1)
    def _():
        other[...] = own[:, :, :HALF]

    column[...] = own[:, :, 0, :]


def load_half(place, own, got, half, sem):
    @pl.when(place[0] == 0)
    def _():
        copy = pltpu.make_async_copy(own.at[:, :, pl.ds(0, HALF)], half, sem)
        copy.start()
        copy.wait()

    @pl.when(place[0] == 1)
    def _():
        copy = pltpu.make_async_copy(got, half, sem)
        copy.start()
        copy.wait()


def run_all(copies):
    for copy in copies:
        copy.start()
    return copies


def wait_all(copies):
    for copy in copies:
        copy.wait()


def send_kernel(place, own, got, column, ybuf):
    def fill(half):
        for z in range(NZ):
            for c in range(4):
                ybuf[z, c * HALF : (c + 1) * HALF] = half(c, z)

    pl.when(place[0] == 0)(lambda: fill(lambda c, z: own[c, z, :HALF]))
    pl.when(place[0] == 1)(lambda: fill(lambda c, z: got[c, z]))
    for c in range(4):
        piece = jnp.where(place[1] == 0, column[c], own[c, :, 0, :])
        for g in range(GY):
            ybuf[g, 4 * HALF + c * NZ : 4 * HALF + (c + 1) * NZ] = piece


def pack_kernel(place, own, got, packed):
    lane = lane_index((HALF, BY))

    def fill(half):
        for z in range(NZ):
            rows = [half(c, z) for c in range(4)]
            for part in range(4):
                total = None
                for c in range(4):
                    shift = 32 * ((c - part) % 4)
                    moved = rows[c] if shift == 0 else pltpu.roll(rows[c], shift, 1)
                    total = moved if total is None else jnp.where(lane >= 32 * c, moved, total)
                packed[4 * z + part] = total

    pl.when(place[0] == 0)(lambda: fill(lambda c, z: own[c, z, :HALF]))
    pl.when(place[0] == 1)(lambda: fill(lambda c, z: got[c, z]))


def blend_kernel(place, yin, source, weight, xbuf_in, xbuf_far, inflow_far,
                 planes, first_near, weight_near, rims, inflow, sem):
    loads = run_all(
        [
            pltpu.make_async_copy(source, first_near, sem.at[0]),
            pltpu.make_async_copy(weight, weight_near, sem.at[1]),
            pltpu.make_async_copy(yin.at[:, pl.ds(4 * HALF, 4 * NZ)], planes, sem.at[2]),
        ]
    )
    wait_all(loads[:2])
    rows = lax.broadcasted_iota(jnp.int32, (NY, BY), 0)
    share = weight_near[...].astype(F32) / 16.0
    first = first_near[...]
    follow = jnp.where(first == NY - 1, 0, first + 1)
    table = jnp.where(rows == first, share, 0.0) + jnp.where(rows == follow, 1.0 - share, 0.0)
    wait_all(loads[2:])
    plane = jnp.concatenate([planes[g] for g in range(GY)], axis=1)
    blended = jnp.dot(plane, table, precision=lax.Precision.HIGHEST, preferred_element_type=F32)
    inflow[...] = blended
    for r in range(4 * NZ):
        rims[r] = jnp.broadcast_to(blended[r : r + 1], (8, BY))
    wait_all(
        run_all(
            [
                pltpu.make_async_copy(rims, xbuf_far.at[:, pl.ds(HALF, 8)], sem.at[3]),
                pltpu.make_async_copy(inflow, inflow_far, sem.at[4]),
            ]
        )
    )


def span_kernel(place, yin, table_high, table_low, yout, both):
    lines = 4 * HALF
    for g in range(GY):
        at = slice(g * BY, (g + 1) * BY)
        both[:lines, at], both[lines:, at] = halves(yin[g, :lines])
    for i in range(4):
        near = (slice(0, (i + 1) * 256), slice((3 - i) * 256, 1024))
        far = (slice((i + 1) * 256, 1024), slice(0, (3 - i) * 256))
        value = None
        for cells, rows in (near, far)[: 1 if i == 3 else 2]:
            pair = jnp.dot(both[:, cells], table_high[rows], preferred_element_type=F32)
            part = pair[:lines] + pair[lines:]
            part += jnp.dot(both[:lines, cells], table_low[rows], preferred_element_type=F32)
            value = part if value is None else value + part
        for k in range(2):
            g = 2 * i + k
            v = yin[g, HALF : 2 * HALF]
            for c in range(4):
                rows = slice(c * HALF, (c + 1) * HALF)
                yout[g, rows] = (
                    v * value[rows, k * BY : (k + 1) * BY]
                    + value[rows, 256 + k * BY : 256 + (k + 1) * BY]
                )


def chunk_place(m):
    return (m % 2) * GX + m // 2


def line_kernel(place, r0, r1, r2, r3, xin, sh, sl, ah, al, xout, plus, minus):
    for m in range(16):
        a = xin[chunk_place(m)]
        b = xin[chunk_place(m + 16)]
        rows = slice(m * HALF, (m + 1) * HALF)
        plus[rows, :BY], plus[rows, BY:] = halves(a + b)
        minus[rows, :BY], minus[rows, BY:] = halves(a - b)
    for ready in (r0, r1, r2, r3):
        ready()
    lane = lane_index((HALF, BY))
    for i in range(4):

        def product(table_high, table_low, both, cells, columns):
            pair = jnp.dot(table_high[:, columns], both[cells], preferred_element_type=F32)
            value = pair[:, :BY] + pair[:, BY:]
            return value + jnp.dot(
                table_low[:, columns], both[cells, :BY], preferred_element_type=F32
            )

        near = (slice(0, (i + 1) * 256), slice((3 - i) * 256, 1024))
        far = (slice((i + 1) * 256, 1024), slice(0, (3 - i) * 256))
        even = product(sh, sl, plus, *near)
        odd = product(ah, al, minus, *near)
        if i < 3:
            even = even + product(sh, sl, plus, *far)
            odd = odd - product(ah, al, minus, *far)
        for k in range(4):
            for side, value in ((0, even + odd), (1, even - odd)):
                place_of = chunk_place(4 * i + k + 16 * side)
                u = jnp.where(lane < 32, xin[place_of], 0.0)
                u = u + pltpu.roll(u, 32, 1)
                u = u + pltpu.roll(u, 64, 1)
                rows = slice(k * HALF, (k + 1) * HALF)
                late = slice(256 + k * HALF, 256 + (k + 1) * HALF)
                xout[place_of, :HALF] = (1.0 + u) * value[rows] + value[late]


def base_kernel(place, own, got, xback_far, base_far, row_far, half, xback, rim, base, row, sem):
    loads = run_all(
        [
            pltpu.make_async_copy(xback_far.at[:, pl.ds(0, HALF)], xback, sem.at[1]),
            pltpu.make_async_copy(xback_far.at[NX // 2 // BX, pl.ds(HALF, 8)], rim, sem.at[2]),
        ]
    )
    load_half(place, own, got, half, sem.at[0])
    wait_all(loads)
    row[...] = rim[:1]
    stores = run_all([pltpu.make_async_copy(row, row_far, sem.at[3])])
    lane = lane_index((HALF, BY))
    for z in range(NZ):
        for c in range(4):
            total = None
            for part in range(4):
                shift = 32 * ((part - c) % 4)
                tile = xback[4 * z + part]
                moved = tile if shift == 0 else pltpu.roll(tile, shift, 1)
                total = moved if total is None else jnp.where(lane >= 32 * part, moved, total)
            q = half[c, z]
            upper = half[c, min(z + 1, NZ - 1)]
            lower = half[c, max(z - 1, 0)]
            mixed = 0.02 * (upper + lower - 2.0 * q) - 0.1 * half[2, z] * (upper - lower)
            base[z, c * HALF : (c + 1) * HALF] = q + total + mixed
    stores += run_all([pltpu.make_async_copy(base, base_far, sem.at[4])])
    wait_all(stores)


def finish_kernel(place, base_far, yback_far, joined_in, send_in, joined, send,
                  base, yback, out, sem):
    pairs = [pl.ds(2 * k, 2) for k in range(4)]
    loads = [
        run_all(
            [
                pltpu.make_async_copy(base_far.at[at], base.at[at], sem.at[k]),
                pltpu.make_async_copy(yback_far.at[at], yback.at[at], sem.at[4 + k]),
            ]
        )
        for k, at in enumerate(pairs)
    ]
    to_own, to_other = [], []
    for k, at in enumerate(pairs):
        piece = out.at[:, at]
        to_own.append(
            pltpu.make_async_copy(piece, joined.at[:, at, pl.ds(0, HALF)], sem.at[8 + k])
        )
        to_other.append(pltpu.make_async_copy(piece, send.at[:, at], sem.at[8 + k]))
    for k in range(4):
        wait_all(loads[k])
        for z in (2 * k, 2 * k + 1):
            for c in range(4):
                rows = slice(c * HALF, (c + 1) * HALF)
                out[c, z] = base[z, rows] + yback[z, rows]
        pl.when(place[0] == 0)(to_own[k].start)
        pl.when(place[0] == 1)(to_other[k].start)
    pl.when(place[0] == 0)(lambda: wait_all(to_own))
    pl.when(place[0] == 1)(lambda: wait_all(to_other))


def join_kernel(place, theirs, joined_in, joined, sem):
    def copies(start):
        return [
            pltpu.make_async_copy(theirs.at[c], joined.at[c, :, pl.ds(start, HALF)], sem.at[c])
            for c in range(4)
        ]

    pl.when(place[0] == 0)(lambda: wait_all(run_all(copies(HALF))))
    pl.when(place[0] == 1)(lambda: wait_all(run_all(copies(0))))


def turn_kernel(place, own, got, mask_far, cells_far, drag_far, row_low_far, row_high_far,
                col_low_far, col_high_far,
                farm, mask, cells, drag, row_low, row_high, col_low, col_high, sem):
    at_x = pl.ds(pl.multiple_of(place[0] * FX, FX), FX)
    mask_load = pltpu.make_async_copy(mask_far.at[:, at_x], mask, sem.at[1])
    mask_load.start()

    @pl.when(place[0] == 0)
    def _():
        copy = pltpu.make_async_copy(got, farm, sem.at[0])
        copy.start()
        copy.wait()

    @pl.when(place[0] == 1)
    def _():
        copy = pltpu.make_async_copy(own.at[:, :, pl.ds(FX, FX)], farm, sem.at[0])
        copy.start()
        copy.wait()

    stores = []
    for c in range(4):
        for z in range(NZ):
            cells[c, pl.ds(z, FX, stride=NZ), :] = farm[c, z]
        stores += run_all([pltpu.make_async_copy(cells.at[c], cells_far.at[c], sem.at[2 + c])])
    mask_load.wait()
    for z in range(NZ):
        drag[pl.ds(z, FX, stride=NZ), :] = mask[z].astype(F32)
    stores += run_all([pltpu.make_async_copy(drag, drag_far, sem.at[6])])
    for c in range(4):
        row_low[c] = cells[c, :NZ]
        row_high[c] = cells[c, (FX - 1) * NZ :]
    lane = lane_index((NZ, BY))

    def step(x, carry):
        low, high = carry
        hit = lane == x
        at = pl.ds(pl.multiple_of(x * NZ, NZ), NZ)
        low = tuple(jnp.where(hit, cells[c, at, 0:1], low[c]) for c in range(4))
        high = tuple(jnp.where(hit, cells[c, at, BY - 1 :], high[c]) for c in range(4))
        return low, high

    zero = tuple(jnp.zeros((NZ, BY), F32) for _ in range(4))
    low, high = lax.fori_loop(0, FX, step, (zero, zero), unroll=4)
    for c in range(4):
        col_low[c] = low[c]
        col_high[c] = high[c]
    pairs = (
        (row_low, row_low_far), (row_high, row_high_far),
        (col_low, col_low_far), (col_high, col_high_far),
    )
    stores += run_all([pltpu.make_async_copy(a, b, sem.at[7 + k]) for k, (a, b) in enumerate(pairs)])
    wait_all(stores)


def above_below(p):
    z = lax.broadcasted_iota(jnp.int32, p.shape, p.ndim - 2)
    above = jnp.where(z == NZ - 1, p, pltpu.roll(p, NZ - 1, p.ndim - 2))
    below = jnp.where(z == 0, p, pltpu.roll(p, 1, p.ndim - 2))
    return above, below


def star_kernel(place, cells, drag, ghost_w, ghost_e, ghost_s, ghost_n, inflow,
                star, partial, strip_s, strip_n, wide):
    first = place[2] == 1
    last = place[3] == 1
    lane = lane_index((NZ, BY))
    level = lax.broadcasted_iota(jnp.int32, (NZ, BY), 0)

    def star_row(x, west_of, east_of):
        u = cells[0, x]
        v = 0.5 * cells[1, x]
        w = 0.5 * cells[2, x]
        fast = 0.5 * (1.0 + u)
        push = drag[x] * jnp.abs(u)
        for c in range(4):
            f = cells[c, x]
            west = west_of(c)
            east = east_of(c)
            north = jnp.where(
                lane == BY - 1,
                pltpu.roll(ghost_n[c], BY - 1 - x, 1),
                pltpu.roll(f, BY - 1, 1),
            )
            south = jnp.where(
                lane == 0, pltpu.roll(ghost_s[c], (BY - x) % BY, 1), pltpu.roll(f, 1, 1)
            )
            above, below = above_below(f)
            moving = -fast * (east - west) - v * (north - south) - w * (above - below)
            mixing = 0.05 * (east + west + north + south - 4.0 * f) + 0.1 * (
                above + below - 2.0 * f
            )
            total = moving + mixing
            if c < 3:
                total = total - push * f
            star[c, x] = f + 0.2 * total

    star_row(
        0, lambda c: jnp.where(first, inflow[c], ghost_w[c]), lambda c: cells[c, 1]
    )

    def star_rows(x, carry):
        star_row(x, lambda c: cells[c, x - 1], lambda c: cells[c, x + 1])
        return carry

    lax.fori_loop(1, FX - 3, star_rows, 0, unroll=6)
    for x in (FX - 3, FX - 2):
        star_rows(x, 0)
    star_row(
        FX - 1,
        lambda c: cells[c, FX - 2],
        lambda c: jnp.where(last, cells[c, FX - 1], ghost_e[c]),
    )

    def source_row(x, west, east):
        v = star[1, x]
        north = jnp.where(lane == BY - 1, 0.0, pltpu.roll(v, BY - 1, 1))
        south = jnp.where(lane == 0, 0.0, pltpu.roll(v, 1, 1))
        w = star[2, x]
        above = jnp.where(level == NZ - 1, 0.0, pltpu.roll(w, NZ - 1, 0))
        below = jnp.where(level == 0, 0.0, pltpu.roll(w, 1, 0))
        total = -0.5 * ((east - west) + (north - south) + (above - below))
        partial[x] = total
        wide[0, x] = jnp.where(lane == HALF - 1, v[:, 0:1], total)
        wide[1, x] = jnp.where(lane == HALF, v[:, BY - 1 :], total)

    source_row(0, jnp.where(first, inflow[0], 0.0), star[0, 1])

    def source_rows(x, carry):
        source_row(x, star[0, x - 1], star[0, x + 1])
        return carry

    lax.fori_loop(1, FX - 3, source_rows, 0, unroll=6)
    for x in (FX - 3, FX - 2):
        source_rows(x, 0)
    source_row(FX - 1, star[0, FX - 2], jnp.where(last, star[0, FX - 1], 0.0))
    for k in range(2):
        wide[k, FX] = star[0, 0]
        wide[k, FX + 1] = star[0, FX - 1]

    def fold(k, carry):
        early_s, late_s = wide[0, k], wide[0, k + FOLD]
        strip_s[k] = jnp.where(lane < HALF, early_s, pltpu.roll(late_s, HALF, 1))
        early_n, late_n = wide[1, k], wide[1, k + FOLD]
        strip_n[k] = jnp.where(lane < HALF, pltpu.roll(early_n, HALF, 1), late_n)
        return carry

    lax.fori_loop(0, FOLD, fold, 0, unroll=11)


def widen_kernel(place, partial, star, from_s, from_n, whole, rims, send_w, send_e):
    lane = lane_index((NZ, BY))
    near = lane < HALF

    def pieces(k, early, own):
        s, n = from_s[k], from_n[k]
        if early:
            n = pltpu.roll(n, HALF, 1)
        else:
            s = pltpu.roll(s, HALF, 1)
        turned = pltpu.roll(own, HALF, 1)
        return jnp.where(near, s, turned), jnp.where(near, turned, n)

    def rows(offset, early):
        def step(k, carry):
            x = k + offset
            a, b = pieces(k, early, partial[x])
            v = 0.5 * star[1, x]
            a = a + jnp.where(lane == HALF, 0.5 * a[:, 0:1], 0.0)
            a = a - jnp.where(lane == HALF - 1, v[:, 0:1], 0.0)
            b = b - jnp.where(lane == HALF - 1, 0.5 * b[:, BY - 1 :], 0.0)
            b = b + jnp.where(lane == HALF, v[:, BY - 1 :], 0.0)
            whole[x, :, :BY] = a
            whole[x, :, BY:] = b
            return carry

        return step

    for k in range(2):
        a, b = pieces(FX + k - FOLD, False, star[0, k * (FX - 1)])
        rims[k, :, :BY] = a
        rims[k, :, BY:] = b
    lax.fori_loop(0, FOLD, rows(0, True), 0, unroll=11)
    lax.fori_loop(0, FX - FOLD, rows(FOLD, False), 0, unroll=31)
    send_w[:HALO] = whole[:HALO]
    send_w[HALO] = rims[0]
    send_e[:HALO] = whole[FX - HALO :]
    send_e[HALO] = rims[1]


def loop_rows(start, count, body):
    trips = count // 4
    unroll = trips if trips <= 19 else max(d for d in range(1, 8) if trips % d == 0)

    def step(k, carry):
        body(start + 4 * k)
        return carry

    lax.fori_loop(0, trips, step, 0, unroll=unroll)


def pressure_kernel(place, whole_far, star_far, rims_far, from_w_far, from_e_far, joined, send,
                  star, rims, far_rims, out, b0, p0, q0, b1, q1, b2, q2, b3, q3, turned, sem):
    pairs = (
        (from_w_far.at[pl.ds(0, HALO)], b0.at[pl.ds(0, HALO)]),
        (whole_far, b0.at[pl.ds(HALO, FX)]),
        (from_e_far.at[pl.ds(0, HALO)], b0.at[pl.ds(HALO + FX, HALO)]),
        (rims_far, rims),
        (from_w_far.at[HALO], far_rims.at[0]),
        (from_e_far.at[HALO], far_rims.at[1]),
    )
    loads = run_all([pltpu.make_async_copy(a, b, sem.at[k]) for k, (a, b) in enumerate(pairs)])
    (star_load,) = run_all([pltpu.make_async_copy(star_far, star, sem.at[6])])
    wait_all(loads)
    targets = [b0, b1, b2, b3]
    results = [q0, q1, q2, q3]

    first = place[2] == 1
    last = place[3] == 1
    b0[HALO] = b0[HALO] + 0.5 * far_rims[0]
    b0[HALO - 1] = b0[HALO - 1] - 0.5 * rims[0]
    b0[HALO + FX - 1] = b0[HALO + FX - 1] - 0.5 * far_rims[1]
    b0[HALO + FX] = b0[HALO + FX] + 0.5 * rims[1]

    def ghosts(p, level):
        low = HALO >> level
        high = low + (FX >> level)

        @pl.when(first)
        def _():
            p[low - 1] = p[low]

        @pl.when(last)
        def _():
            p[high] = jnp.zeros((NZ, 2 * BY), F32)

    def around(rows, level):
        mid = rows[1:5]
        gap = 1 << level
        side = rows[2:6] + rows[0:4] + pltpu.roll(mid, 2 * BY - gap, 2) + pltpu.roll(mid, gap, 2)
        above, below = above_below(mid)
        return mid, 0.25**level * side + (above + below)

    def diagonal(level):
        return 4.0 * 0.25**level + 2.0

    def each(level, halo, body):
        loop_rows((HALO >> level) - halo, (FX >> level) + 2 * halo, body)

    def scaled(b, level):
        scale = 0.8 / diagonal(level)
        return lambda r: scale * b[pl.ds(r - 1, 6)]

    def plain(p):
        return lambda r: p[pl.ds(r - 1, 6)]

    def raised(rows_of, e):
        def rows(r):
            add = e[pl.ds(r // 2 - 1, 4)]
            add = jnp.broadcast_to(add[:, None], (4, 2, NZ, 2 * BY)).reshape(8, NZ, 2 * BY)
            return rows_of(r) + add[1:7]

        return rows

    def sweep(rows_of, q, level, halo):
        b = targets[level]
        scale = 0.8 / diagonal(level)

        def rows(r):
            mid, near = around(rows_of(r), level)
            at = pl.ds(r, 4)
            q[at] = 0.2 * mid + scale * (b[at] + near)

        each(level, halo, rows)

    def descend(rows_of, level, halo):
        b = targets[level]
        coarse = targets[level + 1]
        gap = 1 << level

        def rows(r):
            mid, near = around(rows_of(r), level)
            rest = b[pl.ds(r, 4)] - diagonal(level) * mid + near
            rest = rest.reshape(2, 2, NZ, 2 * BY)
            pair = rest[:, 0] + rest[:, 1]
            lane = lane_index(pair.shape)
            other = jnp.where(
                (lane & gap) == 0,
                pltpu.roll(pair, 2 * BY - gap, 2),
                pltpu.roll(pair, gap, 2),
            )
            coarse[pl.ds(r // 2, 2)] = 0.25 * (pair + other)

        each(level, halo, rows)
        ghosts(coarse, level + 1)

    def cycle(level, rows_of, down, up):
        if level == 3:
            sweep(rows_of, q3, 3, up[3])
            return
        descend(rows_of, level, down[level])
        cycle(level + 1, scaled(targets[level + 1], level + 1), down, up)
        ghosts(results[level + 1], level + 1)
        sweep(raised(rows_of, results[level + 1]), results[level], level, up[level])

    ghosts(b0, 0)
    cycle(0, scaled(b0, 0), (46, 22, 10), (24, 14, 8, 4))
    ghosts(q0, 0)
    sweep(plain(q0), p0, 0, 24)
    ghosts(p0, 0)
    cycle(0, plain(p0), (24, 10, 4), (4, 2, 2, 2))
    ghosts(q0, 0)

    def final(k, carry):
        r = HALO + 4 * k
        rows = q0[pl.ds(r - 1, 6)]
        mid = rows[1:5]

        def inner(values, shift):
            return pltpu.roll(values, shift, 2)[:, :, :BY]

        grad_x = inner(0.5 * (rows[2:6] - rows[0:4]), 2 * BY - HALF)
        grad_y = 0.5 * (inner(mid, 2 * BY - HALF - 1) - inner(mid, 2 * BY - HALF + 1))
        above, low = above_below(mid)
        grad_z = inner(0.5 * (above - low), 2 * BY - HALF)
        at = pl.ds(4 * k, 4)
        to = pl.ds(pl.multiple_of(4 * NZ * k, 4 * NZ), 4 * NZ)
        turned[0, to] = (star[0, at] - grad_x).reshape(4 * NZ, BY)
        turned[1, to] = (star[1, at] - grad_y).reshape(4 * NZ, BY)
        turned[2, to] = (star[2, at] - grad_z).reshape(4 * NZ, BY)
        turned[3, to] = star[3, at].reshape(4 * NZ, BY)
        return carry

    star_load.wait()
    lax.fori_loop(0, FX // 4, final, 0, unroll=4)
    stores = []
    for c in range(4):
        for z in range(NZ):
            out[c, z] = turned[c, pl.ds(z, FX, stride=NZ), :]
        to_own = pltpu.make_async_copy(out.at[c], joined.at[c, :, pl.ds(FX, FX)], sem.at[7 + c])
        to_other = pltpu.make_async_copy(out.at[c], send.at[c], sem.at[7 + c])
        pl.when(place[0] == 1)(to_own.start)
        pl.when(place[0] == 0)(to_other.start)
        stores.append((to_own, to_other))
    for to_own, to_other in stores:
        pl.when(place[0] == 1)(to_own.wait)
        pl.when(place[0] == 0)(to_other.wait)


def in_step(*arrays):
    return lax.optimization_barrier(arrays)


def along_y(step):
    return [(b, (b + step) % GY) for b in range(GY)]


def along_x(step):
    count = 2 * GX
    return [
        (chunk_place(m), chunk_place(m + step)) for m in range(count) if 0 <= m + step < count
    ]


def vmem(*shapes):
    return [pltpu.VMEM(shape, F32) for shape in shapes]


def on_device(fields, turbine_mask, inflow_source, inflow_weight):
    own = fields[0]
    dom, gx = lax.axis_index("dom"), lax.axis_index("gx")
    first, last = (gx == 0) & (dom == 0), (gx == GX - 1) & (dom == 1)
    place = jnp.stack([dom, gx, first, last]).astype(jnp.int32)
    span_high, span_low = [jnp.asarray(t) for t in span_tables()]
    (sh, sl), (ah, al) = line_tables()
    sh, sl, ah, al = [jnp.asarray(t) for t in (sh, sl, ah, al)]
    block = (4, FX, NZ, BY)
    half_block = (4, NZ, HALF, BY)
    rim = (4, NZ, BY)
    strip = (FOLD, NZ, BY)
    wide_row = (NZ, 2 * BY)
    dma = pltpu.SemaphoreType.DMA
    swap = [(0, 1), (1, 0)]
    x_axes = ("dom", "gx")

    other, column = near_call(lead_kernel, [half_block, rim], 2)(place, own)
    column = lax.ppermute(column, "gx", [(NX // 2 // BX, 0)])
    got = lax.ppermute(other, "dom", swap)
    (packed,) = near_call(pack_kernel, [(32, HALF, BY)], 3)(place, own, got)
    packed, column = in_step(packed, column)
    xin = lax.all_to_all(packed, x_axes, 0, 0, tiled=True)

    cells, drag, row_low, row_high, col_low, col_high = raw_call(
        turn_kernel,
        3,
        [(4, FX * NZ, BY), (FX * NZ, BY)] + [rim] * 4,
        vmem(half_block)
        + [pltpu.VMEM((NZ, FX, BY), jnp.int32)]
        + vmem((4, FX * NZ, BY), (FX * NZ, BY), rim, rim, rim, rim)
        + [dma((11,))],
    )(place, own, got, turbine_mask)
    cells = cells.reshape(block)
    drag = drag.reshape(FX, NZ, BY)
    (ybuf,) = near_call(send_kernel, [(GY, 288, BY)], 2)(place, own, got, column)
    ybuf, cells, drag, row_low, row_high, col_low, col_high = in_step(
        ybuf, cells, drag, row_low, row_high, col_low, col_high
    )
    yin = lax.all_to_all(ybuf, "gy", 0, 0, tiled=True)
    ghost_e = lax.ppermute(row_low, x_axes, along_x(-1))
    ghost_w = lax.ppermute(row_high, x_axes, along_x(1))
    ghost_n = lax.ppermute(col_low, "gy", along_y(-1))
    ghost_s = lax.ppermute(col_high, "gy", along_y(1))
    ins = (xin, sh, sl, ah, al)
    (xout,) = staged_call(
        line_kernel,
        ins,
        [(32, 72, BY)],
        scratch=[pltpu.VMEM((NX // 2, 2 * BY), BF16)] * 2,
        late=(1, 2, 3, 4),
    )(place, *ins)
    yin, xout, ghost_e, ghost_w, ghost_n, ghost_s = in_step(
        yin, xout, ghost_e, ghost_w, ghost_n, ghost_s
    )
    xout, blended = raw_call(
        blend_kernel,
        4,
        [(32, 72, BY), (4 * NZ, BY)],
        vmem((GY, 4 * NZ, BY))
        + [pltpu.VMEM((1, BY), jnp.int32)] * 2
        + vmem((32, 8, BY), (4 * NZ, BY))
        + [dma((5,))],
        {4: 0},
    )(place, yin, inflow_source[None], inflow_weight[None], xout)
    xback = lax.all_to_all(xout, x_axes, 0, 0, tiled=True)

    outs = [block, (FX, NZ, BY), strip, strip]
    star, partial, strip_s, strip_n = near_call(
        star_kernel, outs, 4, vmem((2, FX + 2, NZ, BY))
    )(place, cells, drag, ghost_w, ghost_e, ghost_s, ghost_n, blended.reshape(rim))
    from_n = lax.ppermute(strip_s, "gy", along_y(-1))
    from_s = lax.ppermute(strip_n, "gy", along_y(1))
    (yout,) = near_call(
        span_kernel, [(GY, 4 * HALF, BY)], 8, [pltpu.VMEM((8 * HALF, NY), BF16)]
    )(place, yin, span_high, span_low)
    yout, from_n, from_s = in_step(yout, from_n, from_s)
    whole, rims, send_w, send_e = near_call(
        widen_kernel,
        [(FX, *wide_row), (2, *wide_row), (HALO + 1, *wide_row), (HALO + 1, *wide_row)],
        2,
    )(place, partial, star, from_s, from_n)
    xback, yout, whole, rims, send_w, send_e = in_step(xback, yout, whole, rims, send_w, send_e)
    yback = lax.all_to_all(yout, "gy", 0, 0, tiled=True)

    from_e = lax.ppermute(send_w, x_axes, along_x(-1))
    from_w = lax.ppermute(send_e, x_axes, along_x(1))
    base, inflow_row = raw_call(
        base_kernel,
        3,
        [(GY, 4 * HALF, BY), (1, BY)],
        vmem(half_block, (32, HALF, BY), (8, BY), (GY, 4 * HALF, BY), (1, BY)) + [dma((5,))],
    )(place, own, got, xback)
    base, from_e, from_w = in_step(base, from_e, from_w)
    joined, send = raw_call(
        pressure_kernel,
        5,
        [(4, NZ, BX, BY), half_block],
        vmem(block, (2, *wide_row), (2, *wide_row), half_block)
        + vmem(*[(EXT >> level, *wide_row) for level in (0, 0, 0, 1, 1, 2, 2, 3, 3)])
        + vmem((4, FX * NZ, BY))
        + [dma((11,))],
    )(place, whole, star, rims, from_w, from_e)

    yback, base, joined, send = in_step(yback, base, joined, send)
    joined, send = raw_call(
        finish_kernel,
        4,
        [(4, NZ, BX, BY), half_block],
        vmem((GY, 4 * HALF, BY), (GY, 4 * HALF, BY), half_block) + [dma((12,))],
        {3: 0, 4: 1},
    )(place, base, yback, joined, send)
    theirs = lax.ppermute(send, "dom", swap)
    (joined,) = pl.pallas_call(
        join_kernel,
        out_shape=[jax.ShapeDtypeStruct((4, NZ, BX, BY), F32)],
        in_specs=[
            pl.BlockSpec(memory_space=pltpu.SMEM),
            pl.BlockSpec(memory_space=pltpu.VMEM),
            pl.BlockSpec(memory_space=pl.ANY),
        ],
        out_specs=[pl.BlockSpec(memory_space=pl.ANY)],
        scratch_shapes=[dma((4,))],
        input_output_aliases={2: 0},
        compiler_params=pltpu.CompilerParams(vmem_limit_bytes=2 * 1024 * 1024),
    )(place, theirs, joined)
    return joined[None], inflow_row


def solution(mesh):
    placed = (P("dom", None, None, "gx", "gy"), P(None, "gx", "gy"), P("gy"), P("gy"))
    return jax.shard_map(
        on_device,
        mesh=mesh,
        in_specs=placed,
        out_specs=(P("dom", None, None, "gx", "gy"), P(("dom", "gx"), "gy")),
        check_vma=False,
    )
```

```python
import functools

import jax
import jax.numpy as jnp
import ml_dtypes
import numpy as np
from jax import lax
from jax.experimental import pallas as pl
from jax.experimental.pallas import tpu as pltpu
from jax.sharding import PartitionSpec as P

NX = 2048
NY = 1024
NZ = 8
BX = 128
BY = 128
HALF = 64
GX = 16
GY = 8
HALO = 48
FX = 64
FOLD = FX // 2 + 1
EXT = FX + 2 * HALO
F32 = jnp.float32
BF16 = jnp.bfloat16
VMEM_BYTES = 63 * 1024 * 1024


def table_entries(length):
    offset = np.arange(length, dtype=np.float64)
    spacing = 2.0 * np.pi / length
    sign = np.where(offset % 2 == 0, 1.0, -1.0)
    angle = np.pi * offset / length
    angle[0] = 1.0
    slope = 0.5 * spacing * sign * np.cos(angle) / np.sin(angle)
    bend = -0.5 * spacing * spacing * sign / np.sin(angle) ** 2
    slope[0] = 0.0
    bend[0] = -np.pi**2 / 3.0 - spacing * spacing / 6.0
    return -0.2 * slope, 0.2 * 0.05 * bend


def split_bf16(table):
    high = table.astype(np.float32).astype(ml_dtypes.bfloat16)
    low = (table - high.astype(np.float64)).astype(np.float32).astype(ml_dtypes.bfloat16)
    return high, low


def span_tables():
    tiles = []
    i = np.arange(256)
    for d in (3, 2, 1, 0):
        index = (256 * d + i[None, :] - i[:, None]) % NY
        tiles.append(np.concatenate([entry[index] for entry in table_entries(NY)], axis=1))
    return split_bf16(np.concatenate(tiles, axis=0))


def line_tables():
    i = np.arange(256)
    both = []
    for sign in (1.0, -1.0):
        tiles = []
        for d in (3, 2, 1, 0):
            index = 256 * d + i[:, None] - i[None, :]
            tiles.append(
                np.concatenate(
                    [
                        0.5 * (entry[index % NX] + sign * entry[(index + NX // 2) % NX])
                        for entry in table_entries(NX)
                    ],
                    axis=0,
                )
            )
        both.append(split_bf16(np.concatenate(tiles, axis=1)))
    return both


def staged_call(body, ins, outs, scratch=(), gate=None, late=()):
    n, m, k = len(ins), len(outs), len(scratch)

    def kernel(place, *refs):
        far_in, far_out = refs[:n], refs[n : n + m]
        near_in = refs[n + m : 2 * n + m]
        near_out = refs[2 * n + m : 2 * n + 2 * m]
        extra = refs[2 * n + 2 * m : 2 * n + 2 * m + k]
        sem_in, sem_out = refs[2 * n + 2 * m + k :]

        def run():
            loads = [
                pltpu.make_async_copy(far_in[i], near_in[i], sem_in.at[i]) for i in range(n)
            ]
            for load in loads:
                load.start()
            for i in range(n):
                if i not in late:
                    loads[i].wait()
            waits = [loads[i].wait for i in late]
            body(place, *waits, *near_in, *near_out, *extra)
            stores = [
                pltpu.make_async_copy(near_out[i], far_out[i], sem_out.at[i]) for i in range(m)
            ]
            for store in stores:
                store.start()
            for store in stores:
                store.wait()

        if gate is None:
            run()
        else:
            pl.when(place[0] == gate)(run)

    return raw_call(
        kernel,
        n,
        outs,
        [pltpu.VMEM(x.shape, x.dtype) for x in ins]
        + [pltpu.VMEM(shape, F32) for shape in outs]
        + list(scratch)
        + [pltpu.SemaphoreType.DMA((n,)), pltpu.SemaphoreType.DMA((m,))],
    )


def raw_call(kernel, count, outs, scratch, aliases=None):
    return pl.pallas_call(
        kernel,
        out_shape=[jax.ShapeDtypeStruct(shape, F32) for shape in outs],
        in_specs=[pl.BlockSpec(memory_space=pltpu.SMEM)]
        + [pl.BlockSpec(memory_space=pl.ANY)] * count,
        out_specs=[pl.BlockSpec(memory_space=pl.ANY)] * len(outs),
        scratch_shapes=list(scratch),
        input_output_aliases=aliases or {},
        compiler_params=pltpu.CompilerParams(vmem_limit_bytes=VMEM_BYTES),
    )


def near_call(body, outs, limit, scratch=()):
    def call(place, *operands):
        return pl.pallas_call(
            body,
            out_shape=[jax.ShapeDtypeStruct(shape, F32) for shape in outs],
            in_specs=[pl.BlockSpec(memory_space=pltpu.SMEM)]
            + [pl.BlockSpec(memory_space=pltpu.VMEM)] * len(operands),
            out_specs=[pl.BlockSpec(memory_space=pltpu.VMEM)] * len(outs),
            scratch_shapes=list(scratch),
            compiler_params=pltpu.CompilerParams(vmem_limit_bytes=limit * 1024 * 1024),
        )(place, *operands)

    return call


def lane_index(shape):
    return lax.broadcasted_iota(jnp.int32, shape, len(shape) - 1)


def halves(values):
    high = values.astype(BF16)
    return high, (values - high.astype(F32)).astype(BF16)


def lead_kernel(place, own, other, column):
    @pl.when(place[0] == 0)
    def _():
        other[...] = own[:, :, HALF:]

    @pl.when(place[0] == 1)
    def _():
        other[...] = own[:, :, :HALF]

    column[...] = own[:, :, 0, :]


def load_half(place, own, got, half, sem):
    @pl.when(place[0] == 0)
    def _():
        copy = pltpu.make_async_copy(own.at[:, :, pl.ds(0, HALF)], half, sem)
        copy.start()
        copy.wait()

    @pl.when(place[0] == 1)
    def _():
        copy = pltpu.make_async_copy(got, half, sem)
        copy.start()
        copy.wait()


def run_all(copies):
    for copy in copies:
        copy.start()
    return copies


def wait_all(copies):
    for copy in copies:
        copy.wait()


def send_kernel(place, own, got, column, ybuf):
    def fill(half):
        for z in range(NZ):
            for c in range(4):
                ybuf[z, c * HALF : (c + 1) * HALF] = half(c, z)

    pl.when(place[0] == 0)(lambda: fill(lambda c, z: own[c, z, :HALF]))
    pl.when(place[0] == 1)(lambda: fill(lambda c, z: got[c, z]))
    for c in range(4):
        piece = jnp.where(place[1] == 0, column[c], own[c, :, 0, :])
        for g in range(GY):
            ybuf[g, 4 * HALF + c * NZ : 4 * HALF + (c + 1) * NZ] = piece


def pack_kernel(place, own, got, packed):
    lane = lane_index((HALF, BY))

    def fill(half):
        for z in range(NZ):
            rows = [half(c, z) for c in range(4)]
            for part in range(4):
                total = None
                for c in range(4):
                    shift = 32 * ((c - part) % 4)
                    moved = rows[c] if shift == 0 else pltpu.roll(rows[c], shift, 1)
                    total = moved if total is None else jnp.where(lane >= 32 * c, moved, total)
                packed[4 * z + part] = total

    pl.when(place[0] == 0)(lambda: fill(lambda c, z: own[c, z, :HALF]))
    pl.when(place[0] == 1)(lambda: fill(lambda c, z: got[c, z]))


def blend_kernel(place, yin, source, weight, xbuf_in, xbuf_far, inflow_far,
                 planes, first_near, weight_near, rims, inflow, sem):
    loads = run_all(
        [
            pltpu.make_async_copy(source, first_near, sem.at[0]),
            pltpu.make_async_copy(weight, weight_near, sem.at[1]),
            pltpu.make_async_copy(yin.at[:, pl.ds(4 * HALF, 4 * NZ)], planes, sem.at[2]),
        ]
    )
    wait_all(loads[:2])
    rows = lax.broadcasted_iota(jnp.int32, (NY, BY), 0)
    share = weight_near[...].astype(F32) / 16.0
    first = first_near[...]
    follow = jnp.where(first == NY - 1, 0, first + 1)
    table = jnp.where(rows == first, share, jnp.where(rows == follow, 1.0 - share, 0.0))
    table = table.astype(BF16)
    wait_all(loads[2:])
    plane = jnp.concatenate([planes[g] for g in range(GY)], axis=1)
    high, rest = halves(plane)
    middle = plane - high.astype(F32)
    low = (middle - rest.astype(F32)).astype(BF16)
    parts = jnp.dot(
        jnp.concatenate([high, rest, low], axis=0), table, preferred_element_type=F32
    )
    blended = parts[: 4 * NZ] + (parts[4 * NZ : 8 * NZ] + parts[8 * NZ :])
    inflow[...] = blended
    for r in range(4 * NZ):
        rims[r] = jnp.broadcast_to(blended[r : r + 1], (8, BY))
    wait_all(
        run_all(
            [
                pltpu.make_async_copy(rims, xbuf_far.at[:, pl.ds(HALF, 8)], sem.at[3]),
                pltpu.make_async_copy(inflow, inflow_far, sem.at[4]),
            ]
        )
    )


def span_kernel(place, yin, table_high, table_low, yout, both):
    lines = 4 * HALF
    for g in range(GY):
        at = slice(g * BY, (g + 1) * BY)
        both[:lines, at], both[lines:, at] = halves(yin[g, :lines])
    for i in range(4):
        near = (slice(0, (i + 1) * 256), slice((3 - i) * 256, 1024))
        far = (slice((i + 1) * 256, 1024), slice(0, (3 - i) * 256))
        value = None
        for cells, rows in (near, far)[: 1 if i == 3 else 2]:
            pair = jnp.dot(both[:, cells], table_high[rows], preferred_element_type=F32)
            part = pair[:lines] + pair[lines:]
            part += jnp.dot(both[:lines, cells], table_low[rows], preferred_element_type=F32)
            value = part if value is None else value + part
        for k in range(2):
            g = 2 * i + k
            v = yin[g, HALF : 2 * HALF]
            for c in range(4):
                rows = slice(c * HALF, (c + 1) * HALF)
                yout[g, rows] = (
                    v * value[rows, k * BY : (k + 1) * BY]
                    + value[rows, 256 + k * BY : 256 + (k + 1) * BY]
                )


def chunk_place(m):
    return (m % 2) * GX + m // 2


def line_kernel(place, r0, r1, r2, r3, xin, sh, sl, ah, al, xout, plus, minus):
    for m in range(16):
        a = xin[chunk_place(m)]
        b = xin[chunk_place(m + 16)]
        rows = slice(m * HALF, (m + 1) * HALF)
        plus[rows, :BY], plus[rows, BY:] = halves(a + b)
        minus[rows, :BY], minus[rows, BY:] = halves(a - b)
    for ready in (r0, r1, r2, r3):
        ready()
    lane = lane_index((HALF, BY))
    for i in range(4):

        def product(table_high, table_low, both, cells, columns):
            pair = jnp.dot(table_high[:, columns], both[cells], preferred_element_type=F32)
            value = pair[:, :BY] + pair[:, BY:]
            return value + jnp.dot(
                table_low[:, columns], both[cells, :BY], preferred_element_type=F32
            )

        near = (slice(0, (i + 1) * 256), slice((3 - i) * 256, 1024))
        far = (slice((i + 1) * 256, 1024), slice(0, (3 - i) * 256))
        even = product(sh, sl, plus, *near)
        odd = product(ah, al, minus, *near)
        if i < 3:
            even = even + product(sh, sl, plus, *far)
            odd = odd - product(ah, al, minus, *far)
        for k in range(4):
            for side, value in ((0, even + odd), (1, even - odd)):
                place_of = chunk_place(4 * i + k + 16 * side)
                u = jnp.where(lane < 32, xin[place_of], 0.0)
                u = u + pltpu.roll(u, 32, 1)
                u = u + pltpu.roll(u, 64, 1)
                rows = slice(k * HALF, (k + 1) * HALF)
                late = slice(256 + k * HALF, 256 + (k + 1) * HALF)
                xout[place_of, :HALF] = (1.0 + u) * value[rows] + value[late]


def base_kernel(place, own, got, xback_far, base_far, row_far, half, xback, rim, base, row, sem):
    loads = run_all(
        [
            pltpu.make_async_copy(xback_far.at[:, pl.ds(0, HALF)], xback, sem.at[1]),
            pltpu.make_async_copy(xback_far.at[NX // 2 // BX, pl.ds(HALF, 8)], rim, sem.at[2]),
        ]
    )
    load_half(place, own, got, half, sem.at[0])
    wait_all(loads)
    row[...] = rim[:1]
    stores = run_all([pltpu.make_async_copy(row, row_far, sem.at[3])])
    lane = lane_index((HALF, BY))
    for z in range(NZ):
        for c in range(4):
            total = None
            for part in range(4):
                shift = 32 * ((part - c) % 4)
                tile = xback[4 * z + part]
                moved = tile if shift == 0 else pltpu.roll(tile, shift, 1)
                total = moved if total is None else jnp.where(lane >= 32 * part, moved, total)
            q = half[c, z]
            upper = half[c, min(z + 1, NZ - 1)]
            lower = half[c, max(z - 1, 0)]
            mixed = 0.02 * (upper + lower - 2.0 * q) - 0.1 * half[2, z] * (upper - lower)
            base[z, c * HALF : (c + 1) * HALF] = q + total + mixed
    stores += run_all([pltpu.make_async_copy(base, base_far, sem.at[4])])
    wait_all(stores)


def finish_kernel(place, base_far, yback_far, joined_in, send_in, joined, send,
                  base, yback, out, sem):
    pairs = [pl.ds(2 * k, 2) for k in range(4)]
    loads = [
        run_all(
            [
                pltpu.make_async_copy(base_far.at[at], base.at[at], sem.at[k]),
                pltpu.make_async_copy(yback_far.at[at], yback.at[at], sem.at[4 + k]),
            ]
        )
        for k, at in enumerate(pairs)
    ]
    to_own, to_other = [], []
    for k, at in enumerate(pairs):
        piece = out.at[:, at]
        to_own.append(
            pltpu.make_async_copy(piece, joined.at[:, at, pl.ds(0, HALF)], sem.at[8 + k])
        )
        to_other.append(pltpu.make_async_copy(piece, send.at[:, at], sem.at[8 + k]))
    for k in range(4):
        wait_all(loads[k])
        for z in (2 * k, 2 * k + 1):
            for c in range(4):
                rows = slice(c * HALF, (c + 1) * HALF)
                out[c, z] = base[z, rows] + yback[z, rows]
        pl.when(place[0] == 0)(to_own[k].start)
        pl.when(place[0] == 1)(to_other[k].start)
    pl.when(place[0] == 0)(lambda: wait_all(to_own))
    pl.when(place[0] == 1)(lambda: wait_all(to_other))


def join_kernel(place, theirs, joined_in, joined, sem):
    def copies(start):
        return [
            pltpu.make_async_copy(theirs.at[c], joined.at[c, :, pl.ds(start, HALF)], sem.at[c])
            for c in range(4)
        ]

    pl.when(place[0] == 0)(lambda: wait_all(run_all(copies(HALF))))
    pl.when(place[0] == 1)(lambda: wait_all(run_all(copies(0))))


def turn_kernel(place, own, got, mask_far, cells_far, drag_far, row_low_far, row_high_far,
                col_low_far, col_high_far,
                farm, mask, cells, drag, row_low, row_high, col_low, col_high, sem):
    at_x = pl.ds(pl.multiple_of(place[0] * FX, FX), FX)
    mask_load = pltpu.make_async_copy(mask_far.at[:, at_x], mask, sem.at[1])
    mask_load.start()

    @pl.when(place[0] == 0)
    def _():
        copy = pltpu.make_async_copy(got, farm, sem.at[0])
        copy.start()
        copy.wait()

    @pl.when(place[0] == 1)
    def _():
        copy = pltpu.make_async_copy(own.at[:, :, pl.ds(FX, FX)], farm, sem.at[0])
        copy.start()
        copy.wait()

    stores = []
    for c in range(4):
        for z in range(NZ):
            cells[c, pl.ds(z, FX, stride=NZ), :] = farm[c, z]
        stores += run_all([pltpu.make_async_copy(cells.at[c], cells_far.at[c], sem.at[2 + c])])
    mask_load.wait()
    for z in range(NZ):
        drag[pl.ds(z, FX, stride=NZ), :] = mask[z].astype(F32)
    stores += run_all([pltpu.make_async_copy(drag, drag_far, sem.at[6])])
    for c in range(4):
        row_low[c] = cells[c, :NZ]
        row_high[c] = cells[c, (FX - 1) * NZ :]
    lane = lane_index((NZ, BY))

    def step(x, carry):
        low, high = carry
        hit = lane == x
        at = pl.ds(pl.multiple_of(x * NZ, NZ), NZ)
        low = tuple(jnp.where(hit, cells[c, at, 0:1], low[c]) for c in range(4))
        high = tuple(jnp.where(hit, cells[c, at, BY - 1 :], high[c]) for c in range(4))
        return low, high

    zero = tuple(jnp.zeros((NZ, BY), F32) for _ in range(4))
    low, high = lax.fori_loop(0, FX, step, (zero, zero), unroll=4)
    for c in range(4):
        col_low[c] = low[c]
        col_high[c] = high[c]
    pairs = (
        (row_low, row_low_far), (row_high, row_high_far),
        (col_low, col_low_far), (col_high, col_high_far),
    )
    stores += run_all([pltpu.make_async_copy(a, b, sem.at[7 + k]) for k, (a, b) in enumerate(pairs)])
    wait_all(stores)


def above_below(p):
    z = lax.broadcasted_iota(jnp.int32, p.shape, p.ndim - 2)
    above = jnp.where(z == NZ - 1, p, pltpu.roll(p, NZ - 1, p.ndim - 2))
    below = jnp.where(z == 0, p, pltpu.roll(p, 1, p.ndim - 2))
    return above, below


def star_kernel(place, cells, drag, ghost_w, ghost_e, ghost_s, ghost_n, inflow,
                star, partial, strip_s, strip_n, wide):
    first = place[2] == 1
    last = place[3] == 1
    lane = lane_index((NZ, BY))
    level = lax.broadcasted_iota(jnp.int32, (NZ, BY), 0)

    def star_row(x, west_of, east_of):
        u = cells[0, x]
        v = 0.5 * cells[1, x]
        w = 0.5 * cells[2, x]
        fast = 0.5 * (1.0 + u)
        push = drag[x] * jnp.abs(u)
        for c in range(4):
            f = cells[c, x]
            west = west_of(c)
            east = east_of(c)
            north = jnp.where(
                lane == BY - 1,
                pltpu.roll(ghost_n[c], BY - 1 - x, 1),
                pltpu.roll(f, BY - 1, 1),
            )
            south = jnp.where(
                lane == 0, pltpu.roll(ghost_s[c], (BY - x) % BY, 1), pltpu.roll(f, 1, 1)
            )
            above, below = above_below(f)
            moving = -fast * (east - west) - v * (north - south) - w * (above - below)
            mixing = 0.05 * (east + west + north + south - 4.0 * f) + 0.1 * (
                above + below - 2.0 * f
            )
            total = moving + mixing
            if c < 3:
                total = total - push * f
            star[c, x] = f + 0.2 * total

    star_row(
        0, lambda c: jnp.where(first, inflow[c], ghost_w[c]), lambda c: cells[c, 1]
    )

    def star_rows(x, carry):
        star_row(x, lambda c: cells[c, x - 1], lambda c: cells[c, x + 1])
        return carry

    lax.fori_loop(1, FX - 3, star_rows, 0, unroll=6)
    for x in (FX - 3, FX - 2):
        star_rows(x, 0)
    star_row(
        FX - 1,
        lambda c: cells[c, FX - 2],
        lambda c: jnp.where(last, cells[c, FX - 1], ghost_e[c]),
    )

    def source_row(x, west, east):
        v = star[1, x]
        north = jnp.where(lane == BY - 1, 0.0, pltpu.roll(v, BY - 1, 1))
        south = jnp.where(lane == 0, 0.0, pltpu.roll(v, 1, 1))
        w = star[2, x]
        above = jnp.where(level == NZ - 1, 0.0, pltpu.roll(w, NZ - 1, 0))
        below = jnp.where(level == 0, 0.0, pltpu.roll(w, 1, 0))
        total = -0.5 * ((east - west) + (north - south) + (above - below))
        partial[x] = total
        wide[0, x] = jnp.where(lane == HALF - 1, v[:, 0:1], total)
        wide[1, x] = jnp.where(lane == HALF, v[:, BY - 1 :], total)

    source_row(0, jnp.where(first, inflow[0], 0.0), star[0, 1])

    def source_rows(x, carry):
        source_row(x, star[0, x - 1], star[0, x + 1])
        return carry

    lax.fori_loop(1, FX - 3, source_rows, 0, unroll=6)
    for x in (FX - 3, FX - 2):
        source_rows(x, 0)
    source_row(FX - 1, star[0, FX - 2], jnp.where(last, star[0, FX - 1], 0.0))
    for k in range(2):
        wide[k, FX] = star[0, 0]
        wide[k, FX + 1] = star[0, FX - 1]

    def fold(k, carry):
        early_s, late_s = wide[0, k], wide[0, k + FOLD]
        strip_s[k] = jnp.where(lane < HALF, early_s, pltpu.roll(late_s, HALF, 1))
        early_n, late_n = wide[1, k], wide[1, k + FOLD]
        strip_n[k] = jnp.where(lane < HALF, pltpu.roll(early_n, HALF, 1), late_n)
        return carry

    lax.fori_loop(0, FOLD, fold, 0, unroll=11)


def widen_kernel(place, partial, star, from_s, from_n, whole, rims, send_w, send_e):
    lane = lane_index((NZ, BY))
    near = lane < HALF

    def pieces(k, early, own):
        s, n = from_s[k], from_n[k]
        if early:
            n = pltpu.roll(n, HALF, 1)
        else:
            s = pltpu.roll(s, HALF, 1)
        turned = pltpu.roll(own, HALF, 1)
        return jnp.where(near, s, turned), jnp.where(near, turned, n)

    def rows(offset, early):
        def step(k, carry):
            x = k + offset
            a, b = pieces(k, early, partial[x])
            v = 0.5 * star[1, x]
            a = a + jnp.where(lane == HALF, 0.5 * a[:, 0:1], 0.0)
            a = a - jnp.where(lane == HALF - 1, v[:, 0:1], 0.0)
            b = b - jnp.where(lane == HALF - 1, 0.5 * b[:, BY - 1 :], 0.0)
            b = b + jnp.where(lane == HALF, v[:, BY - 1 :], 0.0)
            whole[x, :, :BY] = a
            whole[x, :, BY:] = b
            return carry

        return step

    for k in range(2):
        a, b = pieces(FX + k - FOLD, False, star[0, k * (FX - 1)])
        rims[k, :, :BY] = a
        rims[k, :, BY:] = b
    lax.fori_loop(0, FOLD, rows(0, True), 0, unroll=11)
    lax.fori_loop(0, FX - FOLD, rows(FOLD, False), 0, unroll=31)
    send_w[:HALO] = whole[:HALO]
    send_w[HALO] = rims[0]
    send_e[:HALO] = whole[FX - HALO :]
    send_e[HALO] = rims[1]


def loop_rows(start, count, body):
    trips = count // 4
    unroll = trips if trips <= 19 else max(d for d in range(1, 8) if trips % d == 0)

    def step(k, carry):
        body(start + 4 * k)
        return carry

    lax.fori_loop(0, trips, step, 0, unroll=unroll)


def pressure_kernel(place, whole_far, star_far, rims_far, from_w_far, from_e_far, joined, send,
                  star, rims, far_rims, out, b0, p0, q0, b1, q1, b2, q2, b3, q3, turned, sem):
    pairs = (
        (from_w_far.at[pl.ds(0, HALO)], b0.at[pl.ds(0, HALO)]),
        (whole_far, b0.at[pl.ds(HALO, FX)]),
        (from_e_far.at[pl.ds(0, HALO)], b0.at[pl.ds(HALO + FX, HALO)]),
        (rims_far, rims),
        (from_w_far.at[HALO], far_rims.at[0]),
        (from_e_far.at[HALO], far_rims.at[1]),
    )
    loads = run_all([pltpu.make_async_copy(a, b, sem.at[k]) for k, (a, b) in enumerate(pairs)])
    (star_load,) = run_all([pltpu.make_async_copy(star_far, star, sem.at[6])])
    wait_all(loads)
    targets = [b0, b1, b2, b3]
    results = [q0, q1, q2, q3]

    first = place[2] == 1
    last = place[3] == 1
    b0[HALO] = b0[HALO] + 0.5 * far_rims[0]
    b0[HALO - 1] = b0[HALO - 1] - 0.5 * rims[0]
    b0[HALO + FX - 1] = b0[HALO + FX - 1] - 0.5 * far_rims[1]
    b0[HALO + FX] = b0[HALO + FX] + 0.5 * rims[1]

    def ghosts(p, level):
        low = HALO >> level
        high = low + (FX >> level)

        @pl.when(first)
        def _():
            p[low - 1] = p[low]

        @pl.when(last)
        def _():
            p[high] = jnp.zeros((NZ, 2 * BY), F32)

    def around(rows, level):
        mid = rows[1:5]
        gap = 1 << level
        side = rows[2:6] + rows[0:4] + pltpu.roll(mid, 2 * BY - gap, 2) + pltpu.roll(mid, gap, 2)
        above, below = above_below(mid)
        return mid, 0.25**level * side + (above + below)

    def diagonal(level):
        return 4.0 * 0.25**level + 2.0

    def each(level, halo, body):
        loop_rows((HALO >> level) - halo, (FX >> level) + 2 * halo, body)

    def scaled(b, level):
        scale = 0.8 / diagonal(level)
        return lambda r: scale * b[pl.ds(r - 1, 6)]

    def plain(p):
        return lambda r: p[pl.ds(r - 1, 6)]

    def raised(rows_of, e):
        def rows(r):
            add = e[pl.ds(r // 2 - 1, 4)]
            add = jnp.broadcast_to(add[:, None], (4, 2, NZ, 2 * BY)).reshape(8, NZ, 2 * BY)
            return rows_of(r) + add[1:7]

        return rows

    def sweep(rows_of, q, level, halo):
        b = targets[level]
        scale = 0.8 / diagonal(level)

        def rows(r):
            mid, near = around(rows_of(r), level)
            at = pl.ds(r, 4)
            q[at] = 0.2 * mid + scale * (b[at] + near)

        each(level, halo, rows)

    def descend(rows_of, level, halo):
        b = targets[level]
        coarse = targets[level + 1]
        gap = 1 << level

        def rows(r):
            mid, near = around(rows_of(r), level)
            rest = b[pl.ds(r, 4)] - diagonal(level) * mid + near
            rest = rest.reshape(2, 2, NZ, 2 * BY)
            pair = rest[:, 0] + rest[:, 1]
            lane = lane_index(pair.shape)
            other = jnp.where(
                (lane & gap) == 0,
                pltpu.roll(pair, 2 * BY - gap, 2),
                pltpu.roll(pair, gap, 2),
            )
            coarse[pl.ds(r // 2, 2)] = 0.25 * (pair + other)

        each(level, halo, rows)
        ghosts(coarse, level + 1)

    def cycle(level, rows_of, down, up):
        if level == 3:
            sweep(rows_of, q3, 3, up[3])
            return
        descend(rows_of, level, down[level])
        cycle(level + 1, scaled(targets[level + 1], level + 1), down, up)
        ghosts(results[level + 1], level + 1)
        sweep(raised(rows_of, results[level + 1]), results[level], level, up[level])

    ghosts(b0, 0)
    cycle(0, scaled(b0, 0), (46, 22, 10), (24, 14, 8, 4))
    ghosts(q0, 0)
    sweep(plain(q0), p0, 0, 24)
    ghosts(p0, 0)
    cycle(0, plain(p0), (24, 10, 4), (4, 2, 2, 2))
    ghosts(q0, 0)

    def final(k, carry):
        r = HALO + 4 * k
        rows = q0[pl.ds(r - 1, 6)]
        mid = rows[1:5]

        def inner(values, shift):
            return pltpu.roll(values, shift, 2)[:, :, :BY]

        grad_x = inner(0.5 * (rows[2:6] - rows[0:4]), 2 * BY - HALF)
        grad_y = 0.5 * (inner(mid, 2 * BY - HALF - 1) - inner(mid, 2 * BY - HALF + 1))
        above, low = above_below(mid)
        grad_z = inner(0.5 * (above - low), 2 * BY - HALF)
        at = pl.ds(4 * k, 4)
        to = pl.ds(pl.multiple_of(4 * NZ * k, 4 * NZ), 4 * NZ)
        turned[0, to] = (star[0, at] - grad_x).reshape(4 * NZ, BY)
        turned[1, to] = (star[1, at] - grad_y).reshape(4 * NZ, BY)
        turned[2, to] = (star[2, at] - grad_z).reshape(4 * NZ, BY)
        turned[3, to] = star[3, at].reshape(4 * NZ, BY)
        return carry

    star_load.wait()
    lax.fori_loop(0, FX // 4, final, 0, unroll=4)
    stores = []
    for c in range(4):
        for z in range(NZ):
            out[c, z] = turned[c, pl.ds(z, FX, stride=NZ), :]
        to_own = pltpu.make_async_copy(out.at[c], joined.at[c, :, pl.ds(FX, FX)], sem.at[7 + c])
        to_other = pltpu.make_async_copy(out.at[c], send.at[c], sem.at[7 + c])
        pl.when(place[0] == 1)(to_own.start)
        pl.when(place[0] == 0)(to_other.start)
        stores.append((to_own, to_other))
    for to_own, to_other in stores:
        pl.when(place[0] == 1)(to_own.wait)
        pl.when(place[0] == 0)(to_other.wait)


def in_step(*arrays):
    return lax.optimization_barrier(arrays)


def along_y(step):
    return [(b, (b + step) % GY) for b in range(GY)]


def along_x(step):
    count = 2 * GX
    return [
        (chunk_place(m), chunk_place(m + step)) for m in range(count) if 0 <= m + step < count
    ]


def vmem(*shapes):
    return [pltpu.VMEM(shape, F32) for shape in shapes]


def on_device(fields, turbine_mask, inflow_source, inflow_weight):
    own = fields[0]
    dom, gx = lax.axis_index("dom"), lax.axis_index("gx")
    first, last = (gx == 0) & (dom == 0), (gx == GX - 1) & (dom == 1)
    place = jnp.stack([dom, gx, first, last]).astype(jnp.int32)
    span_high, span_low = [jnp.asarray(t) for t in span_tables()]
    (sh, sl), (ah, al) = line_tables()
    sh, sl, ah, al = [jnp.asarray(t) for t in (sh, sl, ah, al)]
    block = (4, FX, NZ, BY)
    half_block = (4, NZ, HALF, BY)
    rim = (4, NZ, BY)
    strip = (FOLD, NZ, BY)
    wide_row = (NZ, 2 * BY)
    dma = pltpu.SemaphoreType.DMA
    swap = [(0, 1), (1, 0)]
    x_axes = ("dom", "gx")

    other, column = near_call(lead_kernel, [half_block, rim], 2)(place, own)
    column = lax.ppermute(column, "gx", [(NX // 2 // BX, 0)])
    got = lax.ppermute(other, "dom", swap)
    (packed,) = near_call(pack_kernel, [(32, HALF, BY)], 3)(place, own, got)
    packed, column = in_step(packed, column)
    xin = lax.all_to_all(packed, x_axes, 0, 0, tiled=True)

    cells, drag, row_low, row_high, col_low, col_high = raw_call(
        turn_kernel,
        3,
        [(4, FX * NZ, BY), (FX * NZ, BY)] + [rim] * 4,
        vmem(half_block)
        + [pltpu.VMEM((NZ, FX, BY), jnp.int32)]
        + vmem((4, FX * NZ, BY), (FX * NZ, BY), rim, rim, rim, rim)
        + [dma((11,))],
    )(place, own, got, turbine_mask)
    cells = cells.reshape(block)
    drag = drag.reshape(FX, NZ, BY)
    (ybuf,) = near_call(send_kernel, [(GY, 288, BY)], 2)(place, own, got, column)
    ybuf, cells, drag, row_low, row_high, col_low, col_high = in_step(
        ybuf, cells, drag, row_low, row_high, col_low, col_high
    )
    yin = lax.all_to_all(ybuf, "gy", 0, 0, tiled=True)
    ghost_e = lax.ppermute(row_low, x_axes, along_x(-1))
    ghost_w = lax.ppermute(row_high, x_axes, along_x(1))
    ghost_n = lax.ppermute(col_low, "gy", along_y(-1))
    ghost_s = lax.ppermute(col_high, "gy", along_y(1))
    ins = (xin, sh, sl, ah, al)
    (xout,) = staged_call(
        line_kernel,
        ins,
        [(32, 72, BY)],
        scratch=[pltpu.VMEM((NX // 2, 2 * BY), BF16)] * 2,
        late=(1, 2, 3, 4),
    )(place, *ins)
    yin, xout, ghost_e, ghost_w, ghost_n, ghost_s = in_step(
        yin, xout, ghost_e, ghost_w, ghost_n, ghost_s
    )
    xout, blended = raw_call(
        blend_kernel,
        4,
        [(32, 72, BY), (4 * NZ, BY)],
        vmem((GY, 4 * NZ, BY))
        + [pltpu.VMEM((1, BY), jnp.int32)] * 2
        + vmem((32, 8, BY), (4 * NZ, BY))
        + [dma((5,))],
        {4: 0},
    )(place, yin, inflow_source[None], inflow_weight[None], xout)
    xback = lax.all_to_all(xout, x_axes, 0, 0, tiled=True)

    outs = [block, (FX, NZ, BY), strip, strip]
    star, partial, strip_s, strip_n = near_call(
        star_kernel, outs, 4, vmem((2, FX + 2, NZ, BY))
    )(place, cells, drag, ghost_w, ghost_e, ghost_s, ghost_n, blended.reshape(rim))
    from_n = lax.ppermute(strip_s, "gy", along_y(-1))
    from_s = lax.ppermute(strip_n, "gy", along_y(1))
    (yout,) = near_call(
        span_kernel, [(GY, 4 * HALF, BY)], 8, [pltpu.VMEM((8 * HALF, NY), BF16)]
    )(place, yin, span_high, span_low)
    yout, from_n, from_s = in_step(yout, from_n, from_s)
    whole, rims, send_w, send_e = near_call(
        widen_kernel,
        [(FX, *wide_row), (2, *wide_row), (HALO + 1, *wide_row), (HALO + 1, *wide_row)],
        2,
    )(place, partial, star, from_s, from_n)
    xback, yout, whole, rims, send_w, send_e = in_step(xback, yout, whole, rims, send_w, send_e)
    yback = lax.all_to_all(yout, "gy", 0, 0, tiled=True)

    from_e = lax.ppermute(send_w, x_axes, along_x(-1))
    from_w = lax.ppermute(send_e, x_axes, along_x(1))
    base, inflow_row = raw_call(
        base_kernel,
        3,
        [(GY, 4 * HALF, BY), (1, BY)],
        vmem(half_block, (32, HALF, BY), (8, BY), (GY, 4 * HALF, BY), (1, BY)) + [dma((5,))],
    )(place, own, got, xback)
    base, from_e, from_w = in_step(base, from_e, from_w)
    joined, send = raw_call(
        pressure_kernel,
        5,
        [(4, NZ, BX, BY), half_block],
        vmem(block, (2, *wide_row), (2, *wide_row), half_block)
        + vmem(*[(EXT >> level, *wide_row) for level in (0, 0, 0, 1, 1, 2, 2, 3, 3)])
        + vmem((4, FX * NZ, BY))
        + [dma((11,))],
    )(place, whole, star, rims, from_w, from_e)

    yback, base, joined, send = in_step(yback, base, joined, send)
    joined, send = raw_call(
        finish_kernel,
        4,
        [(4, NZ, BX, BY), half_block],
        vmem((GY, 4 * HALF, BY), (GY, 4 * HALF, BY), half_block) + [dma((12,))],
        {3: 0, 4: 1},
    )(place, base, yback, joined, send)
    theirs = lax.ppermute(send, "dom", swap)
    (joined,) = pl.pallas_call(
        join_kernel,
        out_shape=[jax.ShapeDtypeStruct((4, NZ, BX, BY), F32)],
        in_specs=[
            pl.BlockSpec(memory_space=pltpu.SMEM),
            pl.BlockSpec(memory_space=pltpu.VMEM),
            pl.BlockSpec(memory_space=pl.ANY),
        ],
        out_specs=[pl.BlockSpec(memory_space=pl.ANY)],
        scratch_shapes=[dma((4,))],
        input_output_aliases={2: 0},
        compiler_params=pltpu.CompilerParams(vmem_limit_bytes=2 * 1024 * 1024),
    )(place, theirs, joined)
    return joined[None], inflow_row


def solution(mesh):
    placed = (P("dom", None, None, "gx", "gy"), P(None, "gx", "gy"), P("gy"), P("gy"))
    return jax.shard_map(
        on_device,
        mesh=mesh,
        in_specs=placed,
        out_specs=(P("dom", None, None, "gx", "gy"), P(("dom", "gx"), "gy")),
        check_vma=False,
    )
```

```python
import functools

import jax
import jax.numpy as jnp
import ml_dtypes
import numpy as np
from jax import lax
from jax.experimental import pallas as pl
from jax.experimental.pallas import tpu as pltpu
from jax.sharding import PartitionSpec as P

NX = 2048
NY = 1024
NZ = 8
BX = 128
BY = 128
HALF = 64
GX = 16
GY = 8
HALO = 48
FX = 64
FOLD = FX // 2 + 1
EXT = FX + 2 * HALO
F32 = jnp.float32
BF16 = jnp.bfloat16
VMEM_BYTES = 63 * 1024 * 1024


def table_entries(length):
    offset = np.arange(length, dtype=np.float64)
    spacing = 2.0 * np.pi / length
    sign = np.where(offset % 2 == 0, 1.0, -1.0)
    angle = np.pi * offset / length
    angle[0] = 1.0
    slope = 0.5 * spacing * sign * np.cos(angle) / np.sin(angle)
    bend = -0.5 * spacing * spacing * sign / np.sin(angle) ** 2
    slope[0] = 0.0
    bend[0] = -np.pi**2 / 3.0 - spacing * spacing / 6.0
    return -0.2 * slope, 0.2 * 0.05 * bend


def split_bf16(table):
    high = table.astype(np.float32).astype(ml_dtypes.bfloat16)
    low = (table - high.astype(np.float64)).astype(np.float32).astype(ml_dtypes.bfloat16)
    return high, low


def span_tables():
    tiles = []
    i = np.arange(256)
    for d in (3, 2, 1, 0):
        index = (256 * d + i[None, :] - i[:, None]) % NY
        tiles.append(np.concatenate([entry[index] for entry in table_entries(NY)], axis=1))
    return split_bf16(np.concatenate(tiles, axis=0))


def line_tables():
    i = np.arange(256)
    both = []
    for sign in (1.0, -1.0):
        tiles = []
        for d in (3, 2, 1, 0):
            index = 256 * d + i[:, None] - i[None, :]
            tiles.append(
                np.concatenate(
                    [
                        0.5 * (entry[index % NX] + sign * entry[(index + NX // 2) % NX])
                        for entry in table_entries(NX)
                    ],
                    axis=0,
                )
            )
        both.append(split_bf16(np.concatenate(tiles, axis=1)))
    return both


def staged_call(body, ins, outs, scratch=(), gate=None, late=()):
    n, m, k = len(ins), len(outs), len(scratch)

    def kernel(place, *refs):
        far_in, far_out = refs[:n], refs[n : n + m]
        near_in = refs[n + m : 2 * n + m]
        near_out = refs[2 * n + m : 2 * n + 2 * m]
        extra = refs[2 * n + 2 * m : 2 * n + 2 * m + k]
        sem_in, sem_out = refs[2 * n + 2 * m + k :]

        def run():
            loads = [
                pltpu.make_async_copy(far_in[i], near_in[i], sem_in.at[i]) for i in range(n)
            ]
            for load in loads:
                load.start()
            for i in range(n):
                if i not in late:
                    loads[i].wait()
            waits = [loads[i].wait for i in late]
            body(place, *waits, *near_in, *near_out, *extra)
            stores = [
                pltpu.make_async_copy(near_out[i], far_out[i], sem_out.at[i]) for i in range(m)
            ]
            for store in stores:
                store.start()
            for store in stores:
                store.wait()

        if gate is None:
            run()
        else:
            pl.when(place[0] == gate)(run)

    return raw_call(
        kernel,
        n,
        outs,
        [pltpu.VMEM(x.shape, x.dtype) for x in ins]
        + [pltpu.VMEM(shape, F32) for shape in outs]
        + list(scratch)
        + [pltpu.SemaphoreType.DMA((n,)), pltpu.SemaphoreType.DMA((m,))],
    )


def raw_call(kernel, count, outs, scratch, aliases=None):
    return pl.pallas_call(
        kernel,
        out_shape=[jax.ShapeDtypeStruct(shape, F32) for shape in outs],
        in_specs=[pl.BlockSpec(memory_space=pltpu.SMEM)]
        + [pl.BlockSpec(memory_space=pl.ANY)] * count,
        out_specs=[pl.BlockSpec(memory_space=pl.ANY)] * len(outs),
        scratch_shapes=list(scratch),
        input_output_aliases=aliases or {},
        compiler_params=pltpu.CompilerParams(vmem_limit_bytes=VMEM_BYTES),
    )


def near_call(body, outs, limit, scratch=()):
    def call(place, *operands):
        return pl.pallas_call(
            body,
            out_shape=[jax.ShapeDtypeStruct(shape, F32) for shape in outs],
            in_specs=[pl.BlockSpec(memory_space=pltpu.SMEM)]
            + [pl.BlockSpec(memory_space=pltpu.VMEM)] * len(operands),
            out_specs=[pl.BlockSpec(memory_space=pltpu.VMEM)] * len(outs),
            scratch_shapes=list(scratch),
            compiler_params=pltpu.CompilerParams(vmem_limit_bytes=limit * 1024 * 1024),
        )(place, *operands)

    return call


def lane_index(shape):
    return lax.broadcasted_iota(jnp.int32, shape, len(shape) - 1)


def halves(values):
    high = values.astype(BF16)
    return high, (values - high.astype(F32)).astype(BF16)


def lead_kernel(place, own, other, column):
    @pl.when(place[0] == 0)
    def _():
        other[...] = own[:, :, HALF:]

    @pl.when(place[0] == 1)
    def _():
        other[...] = own[:, :, :HALF]

    column[...] = own[:, :, 0, :]


def load_half(place, own, got, half, sem):
    @pl.when(place[0] == 0)
    def _():
        copy = pltpu.make_async_copy(own.at[:, :, pl.ds(0, HALF)], half, sem)
        copy.start()
        copy.wait()

    @pl.when(place[0] == 1)
    def _():
        copy = pltpu.make_async_copy(got, half, sem)
        copy.start()
        copy.wait()


def run_all(copies):
    for copy in copies:
        copy.start()
    return copies


def wait_all(copies):
    for copy in copies:
        copy.wait()


def send_kernel(place, own, got, column, ybuf):
    def fill(half):
        for z in range(NZ):
            for c in range(4):
                ybuf[z, c * HALF : (c + 1) * HALF] = half(c, z)

    pl.when(place[0] == 0)(lambda: fill(lambda c, z: own[c, z, :HALF]))
    pl.when(place[0] == 1)(lambda: fill(lambda c, z: got[c, z]))
    for c in range(4):
        piece = jnp.where(place[1] == 0, column[c], own[c, :, 0, :])
        for g in range(GY):
            ybuf[g, 4 * HALF + c * NZ : 4 * HALF + (c + 1) * NZ] = piece


def pack_kernel(place, own, got, packed):
    lane = lane_index((HALF, BY))

    def fill(half):
        for z in range(NZ):
            rows = [half(c, z) for c in range(4)]
            for part in range(4):
                total = None
                for c in range(4):
                    shift = 32 * ((c - part) % 4)
                    moved = rows[c] if shift == 0 else pltpu.roll(rows[c], shift, 1)
                    total = moved if total is None else jnp.where(lane >= 32 * c, moved, total)
                packed[4 * z + part] = total

    pl.when(place[0] == 0)(lambda: fill(lambda c, z: own[c, z, :HALF]))
    pl.when(place[0] == 1)(lambda: fill(lambda c, z: got[c, z]))


def blend_kernel(place, yin, source, weight, xbuf_in, xbuf_far, inflow_far,
                 planes, first_near, weight_near, rims, inflow, sem):
    loads = run_all(
        [
            pltpu.make_async_copy(source, first_near, sem.at[0]),
            pltpu.make_async_copy(weight, weight_near, sem.at[1]),
            pltpu.make_async_copy(yin.at[:, pl.ds(4 * HALF, 4 * NZ)], planes, sem.at[2]),
        ]
    )
    wait_all(loads[:2])
    rows = lax.broadcasted_iota(jnp.int32, (NY, BY), 0)
    share = weight_near[...].astype(F32) / 16.0
    first = first_near[...]
    follow = jnp.where(first == NY - 1, 0, first + 1)
    table = jnp.where(rows == first, share, jnp.where(rows == follow, 1.0 - share, 0.0))
    table = table.astype(BF16)
    wait_all(loads[2:])
    plane = jnp.concatenate([planes[g] for g in range(GY)], axis=1)
    high, rest = halves(plane)
    middle = plane - high.astype(F32)
    low = (middle - rest.astype(F32)).astype(BF16)
    parts = jnp.dot(
        jnp.concatenate([high, rest, low], axis=0), table, preferred_element_type=F32
    )
    blended = parts[: 4 * NZ] + (parts[4 * NZ : 8 * NZ] + parts[8 * NZ :])
    inflow[...] = blended
    for r in range(4 * NZ):
        rims[r] = jnp.broadcast_to(blended[r : r + 1], (8, BY))
    wait_all(
        run_all(
            [
                pltpu.make_async_copy(rims, xbuf_far.at[:, pl.ds(HALF, 8)], sem.at[3]),
                pltpu.make_async_copy(inflow, inflow_far, sem.at[4]),
            ]
        )
    )


def span_kernel(place, yin, table_high, table_low, yout, both):
    lines = 4 * HALF
    for g in range(GY):
        at = slice(g * BY, (g + 1) * BY)
        both[:lines, at], both[lines:, at] = halves(yin[g, :lines])
    for i in range(4):
        near = (slice(0, (i + 1) * 256), slice((3 - i) * 256, 1024))
        far = (slice((i + 1) * 256, 1024), slice(0, (3 - i) * 256))
        value = None
        for cells, rows in (near, far)[: 1 if i == 3 else 2]:
            pair = jnp.dot(both[:, cells], table_high[rows], preferred_element_type=F32)
            part = pair[:lines] + pair[lines:]
            part += jnp.dot(both[:lines, cells], table_low[rows], preferred_element_type=F32)
            value = part if value is None else value + part
        for k in range(2):
            g = 2 * i + k
            v = yin[g, HALF : 2 * HALF]
            for c in range(4):
                rows = slice(c * HALF, (c + 1) * HALF)
                yout[g, rows] = (
                    v * value[rows, k * BY : (k + 1) * BY]
                    + value[rows, 256 + k * BY : 256 + (k + 1) * BY]
                )


def chunk_place(m):
    return (m % 2) * GX + m // 2


def line_kernel(place, r0, r1, r2, r3, xin, sh, sl, ah, al, xout, plus, minus):
    for m in range(16):
        a = xin[chunk_place(m)]
        b = xin[chunk_place(m + 16)]
        rows = slice(m * HALF, (m + 1) * HALF)
        plus[rows, :BY], plus[rows, BY:] = halves(a + b)
        minus[rows, :BY], minus[rows, BY:] = halves(a - b)
    for ready in (r0, r1, r2, r3):
        ready()
    lane = lane_index((HALF, BY))
    for i in range(4):

        def product(table_high, table_low, both, cells, columns):
            pair = jnp.dot(table_high[:, columns], both[cells], preferred_element_type=F32)
            value = pair[:, :BY] + pair[:, BY:]
            return value + jnp.dot(
                table_low[:, columns], both[cells, :BY], preferred_element_type=F32
            )

        near = (slice(0, (i + 1) * 256), slice((3 - i) * 256, 1024))
        far = (slice((i + 1) * 256, 1024), slice(0, (3 - i) * 256))
        even = product(sh, sl, plus, *near)
        odd = product(ah, al, minus, *near)
        if i < 3:
            even = even + product(sh, sl, plus, *far)
            odd = odd - product(ah, al, minus, *far)
        for k in range(4):
            for side, value in ((0, even + odd), (1, even - odd)):
                place_of = chunk_place(4 * i + k + 16 * side)
                u = jnp.where(lane < 32, xin[place_of], 0.0)
                u = u + pltpu.roll(u, 32, 1)
                u = u + pltpu.roll(u, 64, 1)
                rows = slice(k * HALF, (k + 1) * HALF)
                late = slice(256 + k * HALF, 256 + (k + 1) * HALF)
                xout[place_of, :HALF] = (1.0 + u) * value[rows] + value[late]


def base_kernel(place, own, got, xback_far, base_far, row_far, half, xback, rim, base, row, sem):
    loads = run_all(
        [
            pltpu.make_async_copy(
                xback_far.at[pl.ds(8 * k, 8), pl.ds(0, HALF)],
                xback.at[pl.ds(8 * k, 8)],
                sem.at[1 + k],
            )
            for k in range(4)
        ]
    )
    (last,) = run_all(
        [pltpu.make_async_copy(xback_far.at[NX // 2 // BX, pl.ds(HALF, 8)], rim, sem.at[5])]
    )
    load_half(place, own, got, half, sem.at[0])
    lane = lane_index((HALF, BY))
    stores = []
    for k in range(4):
        loads[k].wait()
        for z in (2 * k, 2 * k + 1):
            w = 0.1 * half[2, z]
            for c in range(4):
                total = None
                for part in range(4):
                    shift = 32 * ((part - c) % 4)
                    tile = xback[4 * z + part]
                    moved = tile if shift == 0 else pltpu.roll(tile, shift, 1)
                    total = moved if total is None else jnp.where(lane >= 32 * part, moved, total)
                q = half[c, z]
                upper = half[c, min(z + 1, NZ - 1)]
                lower = half[c, max(z - 1, 0)]
                mixed = 0.02 * (upper + lower - 2.0 * q) - w * (upper - lower)
                base[z, c * HALF : (c + 1) * HALF] = q + total + mixed
        at = pl.ds(2 * k, 2)
        stores += run_all([pltpu.make_async_copy(base.at[at], base_far.at[at], sem.at[7 + k])])
    last.wait()
    row[...] = rim[:1]
    stores += run_all([pltpu.make_async_copy(row, row_far, sem.at[6])])
    wait_all(stores)


def finish_kernel(place, base_far, yback_far, joined_in, send_in, joined, send,
                  base, yback, out, sem):
    pairs = [pl.ds(2 * k, 2) for k in range(4)]
    loads = [
        run_all(
            [
                pltpu.make_async_copy(base_far.at[at], base.at[at], sem.at[k]),
                pltpu.make_async_copy(yback_far.at[at], yback.at[at], sem.at[4 + k]),
            ]
        )
        for k, at in enumerate(pairs)
    ]
    to_own, to_other = [], []
    for k, at in enumerate(pairs):
        piece = out.at[:, at]
        to_own.append(
            pltpu.make_async_copy(piece, joined.at[:, at, pl.ds(0, HALF)], sem.at[8 + k])
        )
        to_other.append(pltpu.make_async_copy(piece, send.at[:, at], sem.at[8 + k]))
    for k in range(4):
        wait_all(loads[k])
        for z in (2 * k, 2 * k + 1):
            for c in range(4):
                rows = slice(c * HALF, (c + 1) * HALF)
                out[c, z] = base[z, rows] + yback[z, rows]
        pl.when(place[0] == 0)(to_own[k].start)
        pl.when(place[0] == 1)(to_other[k].start)
    pl.when(place[0] == 0)(lambda: wait_all(to_own))
    pl.when(place[0] == 1)(lambda: wait_all(to_other))


def join_kernel(place, theirs, joined_in, joined, sem):
    def copies(start):
        return [
            pltpu.make_async_copy(theirs.at[c], joined.at[c, :, pl.ds(start, HALF)], sem.at[c])
            for c in range(4)
        ]

    pl.when(place[0] == 0)(lambda: wait_all(run_all(copies(HALF))))
    pl.when(place[0] == 1)(lambda: wait_all(run_all(copies(0))))


def turn_kernel(place, own, got, mask_far, cells_far, drag_far, row_low_far, row_high_far,
                col_low_far, col_high_far,
                farm, mask, cells, drag, row_low, row_high, col_low, col_high, sem):
    at_x = pl.ds(pl.multiple_of(place[0] * FX, FX), FX)
    mask_load = pltpu.make_async_copy(mask_far.at[:, at_x], mask, sem.at[1])
    mask_load.start()

    @pl.when(place[0] == 0)
    def _():
        copy = pltpu.make_async_copy(got, farm, sem.at[0])
        copy.start()
        copy.wait()

    @pl.when(place[0] == 1)
    def _():
        copy = pltpu.make_async_copy(own.at[:, :, pl.ds(FX, FX)], farm, sem.at[0])
        copy.start()
        copy.wait()

    stores = []
    for c in range(4):
        for z in range(NZ):
            cells[c, pl.ds(z, FX, stride=NZ), :] = farm[c, z]
        stores += run_all([pltpu.make_async_copy(cells.at[c], cells_far.at[c], sem.at[2 + c])])
    mask_load.wait()
    for z in range(NZ):
        drag[pl.ds(z, FX, stride=NZ), :] = mask[z].astype(F32)
    stores += run_all([pltpu.make_async_copy(drag, drag_far, sem.at[6])])
    for c in range(4):
        row_low[c] = cells[c, :NZ]
        row_high[c] = cells[c, (FX - 1) * NZ :]
    lane = lane_index((NZ, BY))

    def step(x, carry):
        low, high = carry
        hit = lane == x
        at = pl.ds(pl.multiple_of(x * NZ, NZ), NZ)
        low = tuple(jnp.where(hit, cells[c, at, 0:1], low[c]) for c in range(4))
        high = tuple(jnp.where(hit, cells[c, at, BY - 1 :], high[c]) for c in range(4))
        return low, high

    zero = tuple(jnp.zeros((NZ, BY), F32) for _ in range(4))
    low, high = lax.fori_loop(0, FX, step, (zero, zero), unroll=4)
    for c in range(4):
        col_low[c] = low[c]
        col_high[c] = high[c]
    pairs = (
        (row_low, row_low_far), (row_high, row_high_far),
        (col_low, col_low_far), (col_high, col_high_far),
    )
    stores += run_all([pltpu.make_async_copy(a, b, sem.at[7 + k]) for k, (a, b) in enumerate(pairs)])
    wait_all(stores)


def above_below(p):
    z = lax.broadcasted_iota(jnp.int32, p.shape, p.ndim - 2)
    above = jnp.where(z == NZ - 1, p, pltpu.roll(p, NZ - 1, p.ndim - 2))
    below = jnp.where(z == 0, p, pltpu.roll(p, 1, p.ndim - 2))
    return above, below


def star_kernel(place, cells, drag, ghost_w, ghost_e, ghost_s, ghost_n, inflow,
                star, partial, strip_s, strip_n, wide):
    first = place[2] == 1
    last = place[3] == 1
    lane = lane_index((NZ, BY))
    level = lax.broadcasted_iota(jnp.int32, (NZ, BY), 0)

    def star_row(x, west_of, east_of):
        u = cells[0, x]
        v = 0.5 * cells[1, x]
        w = 0.5 * cells[2, x]
        fast = 0.5 * (1.0 + u)
        push = drag[x] * jnp.abs(u)
        for c in range(4):
            f = cells[c, x]
            west = west_of(c)
            east = east_of(c)
            north = jnp.where(
                lane == BY - 1,
                pltpu.roll(ghost_n[c], BY - 1 - x, 1),
                pltpu.roll(f, BY - 1, 1),
            )
            south = jnp.where(
                lane == 0, pltpu.roll(ghost_s[c], (BY - x) % BY, 1), pltpu.roll(f, 1, 1)
            )
            above, below = above_below(f)
            moving = -fast * (east - west) - v * (north - south) - w * (above - below)
            mixing = 0.05 * (east + west + north + south - 4.0 * f) + 0.1 * (
                above + below - 2.0 * f
            )
            total = moving + mixing
            if c < 3:
                total = total - push * f
            star[c, x] = f + 0.2 * total

    star_row(
        0, lambda c: jnp.where(first, inflow[c], ghost_w[c]), lambda c: cells[c, 1]
    )

    def star_rows(x, carry):
        star_row(x, lambda c: cells[c, x - 1], lambda c: cells[c, x + 1])
        return carry

    lax.fori_loop(1, FX - 3, star_rows, 0, unroll=6)
    for x in (FX - 3, FX - 2):
        star_rows(x, 0)
    star_row(
        FX - 1,
        lambda c: cells[c, FX - 2],
        lambda c: jnp.where(last, cells[c, FX - 1], ghost_e[c]),
    )

    def source_row(x, west, east):
        v = star[1, x]
        north = jnp.where(lane == BY - 1, 0.0, pltpu.roll(v, BY - 1, 1))
        south = jnp.where(lane == 0, 0.0, pltpu.roll(v, 1, 1))
        w = star[2, x]
        above = jnp.where(level == NZ - 1, 0.0, pltpu.roll(w, NZ - 1, 0))
        below = jnp.where(level == 0, 0.0, pltpu.roll(w, 1, 0))
        total = -0.5 * ((east - west) + (north - south) + (above - below))
        partial[x] = total
        wide[0, x] = jnp.where(lane == HALF - 1, v[:, 0:1], total)
        wide[1, x] = jnp.where(lane == HALF, v[:, BY - 1 :], total)

    source_row(0, jnp.where(first, inflow[0], 0.0), star[0, 1])

    def source_rows(x, carry):
        source_row(x, star[0, x - 1], star[0, x + 1])
        return carry

    lax.fori_loop(1, FX - 3, source_rows, 0, unroll=6)
    for x in (FX - 3, FX - 2):
        source_rows(x, 0)
    source_row(FX - 1, star[0, FX - 2], jnp.where(last, star[0, FX - 1], 0.0))
    for k in range(2):
        wide[k, FX] = star[0, 0]
        wide[k, FX + 1] = star[0, FX - 1]

    def fold(k, carry):
        early_s, late_s = wide[0, k], wide[0, k + FOLD]
        strip_s[k] = jnp.where(lane < HALF, early_s, pltpu.roll(late_s, HALF, 1))
        early_n, late_n = wide[1, k], wide[1, k + FOLD]
        strip_n[k] = jnp.where(lane < HALF, pltpu.roll(early_n, HALF, 1), late_n)
        return carry

    lax.fori_loop(0, FOLD, fold, 0, unroll=11)


def widen_kernel(place, partial, star, from_s, from_n, whole, rims, send_w, send_e):
    lane = lane_index((NZ, BY))
    near = lane < HALF

    def pieces(k, early, own):
        s, n = from_s[k], from_n[k]
        if early:
            n = pltpu.roll(n, HALF, 1)
        else:
            s = pltpu.roll(s, HALF, 1)
        turned = pltpu.roll(own, HALF, 1)
        return jnp.where(near, s, turned), jnp.where(near, turned, n)

    def rows(offset, early):
        def step(k, carry):
            x = k + offset
            a, b = pieces(k, early, partial[x])
            v = 0.5 * star[1, x]
            a = a + jnp.where(lane == HALF, 0.5 * a[:, 0:1], 0.0)
            a = a - jnp.where(lane == HALF - 1, v[:, 0:1], 0.0)
            b = b - jnp.where(lane == HALF - 1, 0.5 * b[:, BY - 1 :], 0.0)
            b = b + jnp.where(lane == HALF, v[:, BY - 1 :], 0.0)
            whole[x, :, :BY] = a
            whole[x, :, BY:] = b
            return carry

        return step

    for k in range(2):
        a, b = pieces(FX + k - FOLD, False, star[0, k * (FX - 1)])
        rims[k, :, :BY] = a
        rims[k, :, BY:] = b
    lax.fori_loop(0, FOLD, rows(0, True), 0, unroll=11)
    lax.fori_loop(0, FX - FOLD, rows(FOLD, False), 0, unroll=31)
    send_w[:HALO] = whole[:HALO]
    send_w[HALO] = rims[0]
    send_e[:HALO] = whole[FX - HALO :]
    send_e[HALO] = rims[1]


def loop_rows(start, count, body):
    trips = count // 4
    unroll = trips if trips <= 19 else max(d for d in range(1, 8) if trips % d == 0)

    def step(k, carry):
        body(start + 4 * k)
        return carry

    lax.fori_loop(0, trips, step, 0, unroll=unroll)


def pressure_kernel(place, whole_far, star_far, rims_far, from_w_far, from_e_far, joined, send,
                  star, rims, far_rims, out, b0, p0, q0, b1, q1, b2, q2, b3, q3, turned, sem):
    pairs = (
        (from_w_far.at[pl.ds(0, HALO)], b0.at[pl.ds(0, HALO)]),
        (whole_far, b0.at[pl.ds(HALO, FX)]),
        (from_e_far.at[pl.ds(0, HALO)], b0.at[pl.ds(HALO + FX, HALO)]),
        (rims_far, rims),
        (from_w_far.at[HALO], far_rims.at[0]),
        (from_e_far.at[HALO], far_rims.at[1]),
    )
    loads = run_all([pltpu.make_async_copy(a, b, sem.at[k]) for k, (a, b) in enumerate(pairs)])
    (star_load,) = run_all([pltpu.make_async_copy(star_far, star, sem.at[6])])
    wait_all(loads)
    targets = [b0, b1, b2, b3]
    results = [q0, q1, q2, q3]

    first = place[2] == 1
    last = place[3] == 1
    b0[HALO] = b0[HALO] + 0.5 * far_rims[0]
    b0[HALO - 1] = b0[HALO - 1] - 0.5 * rims[0]
    b0[HALO + FX - 1] = b0[HALO + FX - 1] - 0.5 * far_rims[1]
    b0[HALO + FX] = b0[HALO + FX] + 0.5 * rims[1]

    def ghosts(p, level):
        low = HALO >> level
        high = low + (FX >> level)

        @pl.when(first)
        def _():
            p[low - 1] = p[low]

        @pl.when(last)
        def _():
            p[high] = jnp.zeros((NZ, 2 * BY), F32)

    def around(rows, level):
        mid = rows[1:5]
        gap = 1 << level
        side = rows[2:6] + rows[0:4] + pltpu.roll(mid, 2 * BY - gap, 2) + pltpu.roll(mid, gap, 2)
        above, below = above_below(mid)
        return mid, 0.25**level * side + (above + below)

    def diagonal(level):
        return 4.0 * 0.25**level + 2.0

    def each(level, halo, body):
        loop_rows((HALO >> level) - halo, (FX >> level) + 2 * halo, body)

    def scaled(b, level):
        scale = 0.8 / diagonal(level)
        return lambda r: scale * b[pl.ds(r - 1, 6)]

    def plain(p):
        return lambda r: p[pl.ds(r - 1, 6)]

    def raised(rows_of, e):
        def rows(r):
            add = e[pl.ds(r // 2 - 1, 4)]
            add = jnp.broadcast_to(add[:, None], (4, 2, NZ, 2 * BY)).reshape(8, NZ, 2 * BY)
            return rows_of(r) + add[1:7]

        return rows

    def sweep(rows_of, q, level, halo):
        b = targets[level]
        scale = 0.8 / diagonal(level)

        def rows(r):
            mid, near = around(rows_of(r), level)
            at = pl.ds(r, 4)
            q[at] = 0.2 * mid + scale * (b[at] + near)

        each(level, halo, rows)

    def descend(rows_of, level, halo):
        b = targets[level]
        coarse = targets[level + 1]
        gap = 1 << level

        def rows(r):
            mid, near = around(rows_of(r), level)
            rest = b[pl.ds(r, 4)] - diagonal(level) * mid + near
            rest = rest.reshape(2, 2, NZ, 2 * BY)
            pair = rest[:, 0] + rest[:, 1]
            lane = lane_index(pair.shape)
            other = jnp.where(
                (lane & gap) == 0,
                pltpu.roll(pair, 2 * BY - gap, 2),
                pltpu.roll(pair, gap, 2),
            )
            coarse[pl.ds(r // 2, 2)] = 0.25 * (pair + other)

        each(level, halo, rows)
        ghosts(coarse, level + 1)

    def cycle(level, rows_of, down, up):
        if level == 3:
            sweep(rows_of, q3, 3, up[3])
            return
        descend(rows_of, level, down[level])
        cycle(level + 1, scaled(targets[level + 1], level + 1), down, up)
        ghosts(results[level + 1], level + 1)
        sweep(raised(rows_of, results[level + 1]), results[level], level, up[level])

    ghosts(b0, 0)
    cycle(0, scaled(b0, 0), (46, 22, 10), (24, 14, 8, 4))
    ghosts(q0, 0)
    sweep(plain(q0), p0, 0, 24)
    ghosts(p0, 0)
    cycle(0, plain(p0), (24, 10, 4), (4, 2, 2, 2))
    ghosts(q0, 0)

    def final(k, carry):
        r = HALO + 4 * k
        rows = q0[pl.ds(r - 1, 6)]
        mid = rows[1:5]

        def inner(values, shift):
            return pltpu.roll(values, shift, 2)[:, :, :BY]

        grad_x = inner(0.5 * (rows[2:6] - rows[0:4]), 2 * BY - HALF)
        grad_y = 0.5 * (inner(mid, 2 * BY - HALF - 1) - inner(mid, 2 * BY - HALF + 1))
        above, low = above_below(mid)
        grad_z = inner(0.5 * (above - low), 2 * BY - HALF)
        at = pl.ds(4 * k, 4)
        to = pl.ds(pl.multiple_of(4 * NZ * k, 4 * NZ), 4 * NZ)
        turned[0, to] = (star[0, at] - grad_x).reshape(4 * NZ, BY)
        turned[1, to] = (star[1, at] - grad_y).reshape(4 * NZ, BY)
        turned[2, to] = (star[2, at] - grad_z).reshape(4 * NZ, BY)
        turned[3, to] = star[3, at].reshape(4 * NZ, BY)
        return carry

    star_load.wait()
    lax.fori_loop(0, FX // 4, final, 0, unroll=4)
    stores = []
    for c in range(4):
        for z in range(NZ):
            out[c, z] = turned[c, pl.ds(z, FX, stride=NZ), :]
        to_own = pltpu.make_async_copy(out.at[c], joined.at[c, :, pl.ds(FX, FX)], sem.at[7 + c])
        to_other = pltpu.make_async_copy(out.at[c], send.at[c], sem.at[7 + c])
        pl.when(place[0] == 1)(to_own.start)
        pl.when(place[0] == 0)(to_other.start)
        stores.append((to_own, to_other))
    for to_own, to_other in stores:
        pl.when(place[0] == 1)(to_own.wait)
        pl.when(place[0] == 0)(to_other.wait)


def in_step(*arrays):
    return lax.optimization_barrier(arrays)


def along_y(step):
    return [(b, (b + step) % GY) for b in range(GY)]


def along_x(step):
    count = 2 * GX
    return [
        (chunk_place(m), chunk_place(m + step)) for m in range(count) if 0 <= m + step < count
    ]


def vmem(*shapes):
    return [pltpu.VMEM(shape, F32) for shape in shapes]


def on_device(fields, turbine_mask, inflow_source, inflow_weight):
    own = fields[0]
    dom, gx = lax.axis_index("dom"), lax.axis_index("gx")
    first, last = (gx == 0) & (dom == 0), (gx == GX - 1) & (dom == 1)
    place = jnp.stack([dom, gx, first, last]).astype(jnp.int32)
    span_high, span_low = [jnp.asarray(t) for t in span_tables()]
    (sh, sl), (ah, al) = line_tables()
    sh, sl, ah, al = [jnp.asarray(t) for t in (sh, sl, ah, al)]
    block = (4, FX, NZ, BY)
    half_block = (4, NZ, HALF, BY)
    rim = (4, NZ, BY)
    strip = (FOLD, NZ, BY)
    wide_row = (NZ, 2 * BY)
    dma = pltpu.SemaphoreType.DMA
    swap = [(0, 1), (1, 0)]
    x_axes = ("dom", "gx")

    other, column = near_call(lead_kernel, [half_block, rim], 2)(place, own)
    column = lax.ppermute(column, "gx", [(NX // 2 // BX, 0)])
    got = lax.ppermute(other, "dom", swap)
    (packed,) = near_call(pack_kernel, [(32, HALF, BY)], 3)(place, own, got)
    packed, column = in_step(packed, column)
    xin = lax.all_to_all(packed, x_axes, 0, 0, tiled=True)

    cells, drag, row_low, row_high, col_low, col_high = raw_call(
        turn_kernel,
        3,
        [(4, FX * NZ, BY), (FX * NZ, BY)] + [rim] * 4,
        vmem(half_block)
        + [pltpu.VMEM((NZ, FX, BY), jnp.int32)]
        + vmem((4, FX * NZ, BY), (FX * NZ, BY), rim, rim, rim, rim)
        + [dma((11,))],
    )(place, own, got, turbine_mask)
    cells = cells.reshape(block)
    drag = drag.reshape(FX, NZ, BY)
    (ybuf,) = near_call(send_kernel, [(GY, 288, BY)], 2)(place, own, got, column)
    ybuf, cells, drag, row_low, row_high, col_low, col_high = in_step(
        ybuf, cells, drag, row_low, row_high, col_low, col_high
    )
    yin = lax.all_to_all(ybuf, "gy", 0, 0, tiled=True)
    ghost_e = lax.ppermute(row_low, x_axes, along_x(-1))
    ghost_w = lax.ppermute(row_high, x_axes, along_x(1))
    ghost_n = lax.ppermute(col_low, "gy", along_y(-1))
    ghost_s = lax.ppermute(col_high, "gy", along_y(1))
    ins = (xin, sh, sl, ah, al)
    (xout,) = staged_call(
        line_kernel,
        ins,
        [(32, 72, BY)],
        scratch=[pltpu.VMEM((NX // 2, 2 * BY), BF16)] * 2,
        late=(1, 2, 3, 4),
    )(place, *ins)
    yin, xout, ghost_e, ghost_w, ghost_n, ghost_s = in_step(
        yin, xout, ghost_e, ghost_w, ghost_n, ghost_s
    )
    xout, blended = raw_call(
        blend_kernel,
        4,
        [(32, 72, BY), (4 * NZ, BY)],
        vmem((GY, 4 * NZ, BY))
        + [pltpu.VMEM((1, BY), jnp.int32)] * 2
        + vmem((32, 8, BY), (4 * NZ, BY))
        + [dma((5,))],
        {4: 0},
    )(place, yin, inflow_source[None], inflow_weight[None], xout)
    xback = lax.all_to_all(xout, x_axes, 0, 0, tiled=True)

    outs = [block, (FX, NZ, BY), strip, strip]
    star, partial, strip_s, strip_n = near_call(
        star_kernel, outs, 4, vmem((2, FX + 2, NZ, BY))
    )(place, cells, drag, ghost_w, ghost_e, ghost_s, ghost_n, blended.reshape(rim))
    from_n = lax.ppermute(strip_s, "gy", along_y(-1))
    from_s = lax.ppermute(strip_n, "gy", along_y(1))
    (yout,) = near_call(
        span_kernel, [(GY, 4 * HALF, BY)], 8, [pltpu.VMEM((8 * HALF, NY), BF16)]
    )(place, yin, span_high, span_low)
    yout, from_n, from_s = in_step(yout, from_n, from_s)
    whole, rims, send_w, send_e = near_call(
        widen_kernel,
        [(FX, *wide_row), (2, *wide_row), (HALO + 1, *wide_row), (HALO + 1, *wide_row)],
        2,
    )(place, partial, star, from_s, from_n)
    xback, yout, whole, rims, send_w, send_e = in_step(xback, yout, whole, rims, send_w, send_e)
    yback = lax.all_to_all(yout, "gy", 0, 0, tiled=True)

    from_e = lax.ppermute(send_w, x_axes, along_x(-1))
    from_w = lax.ppermute(send_e, x_axes, along_x(1))
    base, inflow_row = raw_call(
        base_kernel,
        3,
        [(GY, 4 * HALF, BY), (1, BY)],
        vmem(half_block, (32, HALF, BY), (8, BY), (GY, 4 * HALF, BY), (1, BY)) + [dma((11,))],
    )(place, own, got, xback)
    base, from_e, from_w = in_step(base, from_e, from_w)
    joined, send = raw_call(
        pressure_kernel,
        5,
        [(4, NZ, BX, BY), half_block],
        vmem(block, (2, *wide_row), (2, *wide_row), half_block)
        + vmem(*[(EXT >> level, *wide_row) for level in (0, 0, 0, 1, 1, 2, 2, 3, 3)])
        + vmem((4, FX * NZ, BY))
        + [dma((11,))],
    )(place, whole, star, rims, from_w, from_e)

    yback, base, joined, send = in_step(yback, base, joined, send)
    joined, send = raw_call(
        finish_kernel,
        4,
        [(4, NZ, BX, BY), half_block],
        vmem((GY, 4 * HALF, BY), (GY, 4 * HALF, BY), half_block) + [dma((12,))],
        {3: 0, 4: 1},
    )(place, base, yback, joined, send)
    theirs = lax.ppermute(send, "dom", swap)
    (joined,) = pl.pallas_call(
        join_kernel,
        out_shape=[jax.ShapeDtypeStruct((4, NZ, BX, BY), F32)],
        in_specs=[
            pl.BlockSpec(memory_space=pltpu.SMEM),
            pl.BlockSpec(memory_space=pltpu.VMEM),
            pl.BlockSpec(memory_space=pl.ANY),
        ],
        out_specs=[pl.BlockSpec(memory_space=pl.ANY)],
        scratch_shapes=[dma((4,))],
        input_output_aliases={2: 0},
        compiler_params=pltpu.CompilerParams(vmem_limit_bytes=2 * 1024 * 1024),
    )(place, theirs, joined)
    return joined[None], inflow_row


def solution(mesh):
    placed = (P("dom", None, None, "gx", "gy"), P(None, "gx", "gy"), P("gy"), P("gy"))
    return jax.shard_map(
        on_device,
        mesh=mesh,
        in_specs=placed,
        out_specs=(P("dom", None, None, "gx", "gy"), P(("dom", "gx"), "gy")),
        check_vma=False,
    )
```
